32 devices in a mesh: row: 4 (over y, x), col: 8 (over z, core).
Axes of the slice: x: 2, y: 2, z: 4, core: 2. Of those that a mesh axis runs over, the one named last changes fastest.
Arguments:
- activations: bfloat16 [64, 8192], P('col', 'row'), may hold values from -6 to 6
- out_grad: bfloat16 [64, 8192], P('col', 'row'), may hold values from -6 to 6
- w_gate: bfloat16 [8192, 28672], P('row', 'col'), may hold values from -0.0625 to 0.0625
- w_up: bfloat16 [8192, 28672], P('row', 'col'), may hold values from -0.0625 to 0.0625
- w_down: bfloat16 [28672, 8192], P('col', 'row'), may hold values from -0.03125 to 0.03125
Outputs:
- grad_input: bfloat16 [64, 8192], P('col', 'row')
- grad_w_gate: bfloat16 [8192, 28672], P('row', 'col')
- grad_w_up: bfloat16 [8192, 28672], P('row', 'col')
- grad_w_down: bfloat16 [28672, 8192], P('col', 'row')
The draws below stay inside these ranges and needn't reach their ends.
All inputs are finite; a program needn't handle non-finite values.
Results may differ from the reference program's by a relative error of at most 0.0049.
Values may be sent and summed in bfloat16 or wider, within the bound.
No kernel may reach another device: no remote copies, remote signals or barrier semaphores. Data moves between devices by JAX's collectives and lax.ppermute only.
A program may use at most 128 MiB of HBM per device.

```python
import jax
import jax.numpy as jnp
from jax import lax

D = 8192
FF = 28672
TOKENS = 64


def shard_levels(stream_key, extent, shards, least, high):
    def one(dim, blocks):
        steps = jax.random.uniform(jax.random.fold_in(jax.random.fold_in(stream_key, 6), dim), (blocks,), jnp.float32, least / len(shards), high / len(shards))
        return jnp.repeat(jnp.exp(steps), extent[dim] // blocks).reshape((-1,) + (1,) * (len(extent) - dim - 1))

    gain = one(*shards[0])
    for cut in shards[1:]:
        gain = gain * one(*cut)
    return gain


def noise(own_key, dims, spread, reach, pieces=(), kind=jnp.bfloat16):
    array = jax.random.normal(own_key, dims, jnp.float32) * spread
    if len(pieces) > 0:
        array = shard_levels(own_key, dims, pieces, -0.22, 0.18) * array
    return jnp.clip(array, min=-reach, max=reach).astype(kind)


def setup_inputs(seed: int = 0) -> dict:
    seeds = jax.random.split(jax.random.key(seed), 6)
    activations = noise(seeds[0], (TOKENS, D), 1.0, 6.0, ((0, 8), (1, 4)))
    out_grad = noise(seeds[1], (TOKENS, D), 1.0, 6.0, ((0, 8), (1, 4)))
    w_gate = noise(seeds[2], (D, FF), D ** -0.5, 0.0625, ((0, 4), (1, 8)))
    w_up = noise(seeds[3], (D, FF), D ** -0.5, 0.0625, ((0, 4), (1, 8)))
    w_down = noise(seeds[4], (FF, D), FF ** -0.5, 0.03125, ((0, 8), (1, 4)))
    return {"activations": activations, "out_grad": out_grad, "w_gate": w_gate, "w_up": w_up, "w_down": w_down}


def reference(activations, out_grad, w_gate, w_up, w_down):
    contract_last = (((1,), (1,)), ((), ()))
    contract_first = (((0,), (0,)), ((), ()))
    gate = jnp.dot(activations, w_gate, preferred_element_type=jnp.float32)
    upward = jnp.dot(activations, w_up, preferred_element_type=jnp.float32)
    back = lax.dot_general(out_grad, w_down, contract_last, preferred_element_type=jnp.float32)
    sigma = jax.nn.sigmoid(gate)
    hidden = (gate * sigma * upward).astype(jnp.bfloat16)
    grad_gate = (back * upward * sigma * (1.0 + gate * (1.0 - sigma))).astype(jnp.bfloat16)
    grad_up = (back * gate * sigma).astype(jnp.bfloat16)
    grad_input = lax.dot_general(grad_gate, w_gate, contract_last, preferred_element_type=jnp.float32)
    grad_input = grad_input + lax.dot_general(grad_up, w_up, contract_last, preferred_element_type=jnp.float32)
    grad_w_gate = lax.dot_general(activations, grad_gate, contract_first, preferred_element_type=jnp.float32)
    grad_w_up = lax.dot_general(activations, grad_up, contract_first, preferred_element_type=jnp.float32)
    grad_w_down = lax.dot_general(hidden, out_grad, contract_first, preferred_element_type=jnp.float32)
    return (grad_input.astype(jnp.bfloat16), grad_w_gate.astype(jnp.bfloat16), grad_w_up.astype(jnp.bfloat16), grad_w_down.astype(jnp.bfloat16))
```

```python
import functools

import jax
import jax.numpy as jnp
from jax import lax
from jax.experimental import pallas as pl
from jax.experimental.pallas import tpu as pltpu
from jax.sharding import PartitionSpec as P

BF16, F32 = jnp.bfloat16, jnp.float32
HBM = pl.BlockSpec(memory_space=pl.ANY)
VMEM = pl.BlockSpec(memory_space=pltpu.VMEM)
SMEM = pl.BlockSpec(memory_space=pltpu.SMEM)
CONTRACT_LAST = (((1,), (1,)), ((), ()))
CONTRACT_FIRST = (((0,), (0,)), ((), ()))
CHUNKS = 2


def params(mib):
    return pltpu.CompilerParams(vmem_limit_bytes=mib << 20)


def tiles(width, tile=512):
    return [(at, min(tile, width - at)) for at in range(0, width, tile)]


def exchange(x, axis, size, offset):
    return lax.ppermute(x, axis, [(i, i ^ offset) for i in range(size)])


def order_kernel(rows, me_ref, mine_ref, other_ref, tokens_ref, grads_ref, scratch):
    me = me_ref[0]
    share = rows // 2
    n = mine_ref.shape[0] // rows
    total = tokens_ref.shape[0]
    per_row = total // scratch.shape[1]
    for half, out in ((0, tokens_ref), (1, grads_ref)):
        for k in range(n):
            for c, ref in ((0, mine_ref), (1, other_ref)):
                block = ref[k * rows : (k + 1) * rows, :].astype(F32)
                at = (2 * k + c) * share
                scratch[half, at // per_row, at % per_row : at % per_row + share, :] = block[
                    half * share : (half + 1) * share
                ]
        parts = [scratch[half, k ^ me] for k in range(scratch.shape[1])]
        out[...] = jnp.concatenate(parts, axis=0).astype(BF16)


def forward_kernel(start, width, own, tokens_ref, grads_ref, gate_ref, up_ref, down_ref, keep_ref, *send_refs):
    tokens, grads = tokens_ref[...], grads_ref[...]
    for at, size in tiles(width):
        cols = slice(start + at, start + at + size)
        gate = jnp.dot(tokens, gate_ref[:, cols], preferred_element_type=F32)
        upward = jnp.dot(tokens, up_ref[:, cols], preferred_element_type=F32)
        back = lax.dot_general(grads, down_ref[cols, :], CONTRACT_LAST, preferred_element_type=F32)
        for i, part in enumerate((gate, upward, back)):
            to = slice(i * width + at, i * width + at + size)
            keep_ref[:, to] = part[:own]
            for s, ref in enumerate(send_refs):
                ref[:, to] = part[(s + 1) * own : (s + 2) * own].astype(BF16)


def swiglu_kernel(width, keep_ref, *refs):
    out_ref = refs[-1]
    sums = keep_ref[...]
    for ref in refs[:-1]:
        sums = sums + ref[...].astype(F32)
    gate, upward, back = (sums[:, i * width : (i + 1) * width] for i in range(3))
    sigma = 1.0 / (1.0 + jnp.exp(-gate))
    out_ref[:, :width] = (back * upward * sigma * (1.0 + gate * (1.0 - sigma))).astype(BF16)
    out_ref[:, width : 2 * width] = (back * gate * sigma).astype(BF16)
    out_ref[:, 2 * width :] = (gate * sigma * upward).astype(BF16)


def input_kernel(start, width, first, last, n, me_ref, *refs):
    pieces, refs = refs[:n], refs[n:]
    gate_ref, up_ref = refs[:2]
    out_ref = refs[-1]
    grads = jnp.concatenate([ref[:, : 2 * width] for ref in pieces], axis=0)
    own = pieces[0].shape[0]
    for at, size in tiles(gate_ref.shape[0]):
        rows = slice(at, at + size)
        part = lax.dot_general(grads[:, :width], gate_ref[rows, start : start + width], CONTRACT_LAST, preferred_element_type=F32)
        part += lax.dot_general(grads[:, width:], up_ref[rows, start : start + width], CONTRACT_LAST, preferred_element_type=F32)
        if not first:
            part += refs[2][:, rows]
        if last:
            for k in range(n):
                out_ref[pl.ds(pl.multiple_of((k ^ me_ref[0]) * own, 8), own), rows] = part[k * own : (k + 1) * own]
        else:
            out_ref[:, rows] = part


def weights_kernel(n, tokens_ref, grads_ref, *refs):
    pieces = refs[: 3 * n]
    g_gate_ref, g_up_ref, g_down_ref = refs[-3:]
    grad_gate, grad_up, hidden = (jnp.concatenate([r[...] for r in pieces[i * n : (i + 1) * n]], axis=0) for i in range(3))
    g_gate_ref[...] = lax.dot_general(tokens_ref[...], grad_gate, CONTRACT_FIRST, preferred_element_type=F32).astype(BF16)
    g_up_ref[...] = lax.dot_general(tokens_ref[...], grad_up, CONTRACT_FIRST, preferred_element_type=F32).astype(BF16)
    g_down_ref[...] = lax.dot_general(hidden, grads_ref[...], CONTRACT_FIRST, preferred_element_type=F32).astype(BF16)


def per_device(n_row, n_col, activations, out_grad, w_gate, w_up, w_down):
    share, depth = activations.shape
    hidden = w_gate.shape[1]
    total = share * n_col
    own = total // n_row
    me = lax.axis_index("row").astype(jnp.int32).reshape(1)
    shape = jax.ShapeDtypeStruct

    mine = jnp.concatenate([activations, out_grad], axis=0)
    near = jnp.concatenate([mine] + [exchange(mine, "col", n_col, 2 * k) for k in range(1, n_col // 2)], axis=0)
    far = exchange(near, "col", n_col, 1)
    tokens, grads = pl.pallas_call(
        functools.partial(order_kernel, 2 * share),
        out_shape=[pltpu.VMEM((total, depth), BF16)] * 2,
        in_specs=[SMEM, VMEM, VMEM],
        out_specs=[VMEM] * 2,
        scratch_shapes=[pltpu.VMEM((2, n_row, own, depth), F32)],
        compiler_params=params(6),
        name="order",
    )(me, near, far)

    w_gate, w_up, w_down = (pltpu.with_memory_space_constraint(w, pltpu.VMEM) for w in (w_gate, w_up, w_down))

    unit = 256 if hidden % 256 == 0 else 128
    cuts = [unit * (hidden // unit * i // CHUNKS) for i in range(CHUNKS + 1)]
    spans = [(a, b - a) for a, b in zip(cuts[:-1], cuts[1:])]

    partial = []
    for start, width in spans:
        keep, *sends = pl.pallas_call(
            functools.partial(forward_kernel, start, width, own),
            out_shape=[pltpu.VMEM((own, 3 * width), F32)] + [pltpu.VMEM((own, 3 * width), BF16)] * (n_row - 1),
            in_specs=[VMEM] * 5,
            out_specs=[VMEM] * n_row,
            compiler_params=params(8),
            name="forward",
        )(tokens, grads, w_gate, w_up, w_down)
        partial.append([keep] + [exchange(x, "row", n_row, s + 1) for s, x in enumerate(sends)])

    pieces = []
    for (start, width), parts in zip(spans, partial):
        mine = pl.pallas_call(
            functools.partial(swiglu_kernel, width),
            out_shape=pltpu.VMEM((own, 3 * width), BF16),
            in_specs=[VMEM] * n_row,
            out_specs=VMEM,
            compiler_params=params(8),
            name="swiglu",
        )(*parts)
        pieces.append([mine] + [exchange(mine, "row", n_row, s) for s in range(1, n_row)])

    grad_input, outs = None, None
    for i, ((start, width), parts) in enumerate(zip(spans, pieces)):
        grad_input = pl.pallas_call(
            functools.partial(input_kernel, start, width, i == 0, i == CHUNKS - 1, n_row),
            out_shape=pltpu.VMEM((total, depth), F32),
            in_specs=[SMEM] + [VMEM] * (n_row + 2 + (i > 0)),
            out_specs=VMEM,
            compiler_params=params(8),
            name="input_grad",
        )(me, *parts, w_gate, w_up, *([grad_input] if i else []))
    for i, ((start, width), parts) in enumerate(zip(spans, pieces)):
        tile = 256 if width % 256 == 0 else 128
        n = width // tile
        first = start // tile
        piece = lambda j: pl.BlockSpec((own, tile), lambda t, j=j: (0, j * n + t))
        outs = pl.pallas_call(
            functools.partial(weights_kernel, n_row),
            grid=(n,),
            out_shape=[shape((depth, hidden), BF16)] * 2 + [shape((hidden, depth), BF16)],
            in_specs=[pl.BlockSpec((total, depth), lambda t: (0, 0))] * 2
            + [piece(j) for j in range(3) for _ in range(n_row)]
            + [HBM] * (3 if i else 0),
            out_specs=[pl.BlockSpec((depth, tile), lambda t: (0, first + t))] * 2
            + [pl.BlockSpec((tile, depth), lambda t: (first + t, 0))],
            input_output_aliases={2 + 3 * n_row + k: k for k in range(3)} if i else {},
            compiler_params=params(14),
            name="weight_grads",
        )(tokens, grads, *(parts * 3), *(outs if i else ()))

    blocks = grad_input.reshape(n_col // 2, 2, share, depth)
    summed = blocks[:, 0] + exchange(blocks[:, 1], "col", n_col, 1)
    result = summed[0]
    for k in range(1, n_col // 2):
        result = result + exchange(summed[k], "col", n_col, 2 * k)
    return (result.astype(BF16), *outs)


def solution(mesh):
    in_specs = (P("col", "row"), P("col", "row"), P("row", "col"), P("row", "col"), P("col", "row"))
    out_specs = (P("col", "row"), P("row", "col"), P("row", "col"), P("col", "row"))
    return jax.shard_map(
        functools.partial(per_device, mesh.shape["row"], mesh.shape["col"]),
        mesh=mesh,
        in_specs=in_specs,
        out_specs=out_specs,
        check_vma=False,
    )
```

```python
import functools

import jax
import jax.numpy as jnp
from jax import lax
from jax.experimental import pallas as pl
from jax.experimental.pallas import tpu as pltpu
from jax.sharding import PartitionSpec as P

BF16, F32 = jnp.bfloat16, jnp.float32
HBM = pl.BlockSpec(memory_space=pl.ANY)
VMEM = pl.BlockSpec(memory_space=pltpu.VMEM)
SMEM = pl.BlockSpec(memory_space=pltpu.SMEM)
CONTRACT_LAST = (((1,), (1,)), ((), ()))
CONTRACT_FIRST = (((0,), (0,)), ((), ()))
PARAMS = pltpu.CompilerParams(vmem_limit_bytes=14 << 20)
vmem = pltpu.VMEM
shape = jax.ShapeDtypeStruct


def exchange(x, axis, size, offset):
    return lax.ppermute(x, axis, [(i, i ^ offset) for i in range(size)])


def tiles(width, tile):
    return [(at, min(tile, width - at)) for at in range(0, width, tile)]


def join_kernel(*refs):
    rows = refs[0].shape[0]
    for i, ref in enumerate(refs[:-2]):
        refs[-1][i * rows : (i + 1) * rows, :] = ref[...]


def order_kernel(rows, me_ref, mine_ref, other_ref, tokens_ref, grads_ref, turned_ref, scratch):
    me = me_ref[0]
    share = rows // 2
    n = mine_ref.shape[0] // rows
    total = tokens_ref.shape[0]
    per_row = total // scratch.shape[1]
    for half, out in ((0, tokens_ref), (1, grads_ref)):
        for k in range(n):
            for c, ref in ((0, mine_ref), (1, other_ref)):
                block = ref[k * rows : (k + 1) * rows, :].astype(F32)
                at = (2 * k + c) * share
                scratch[half, at // per_row, at % per_row : at % per_row + share, :] = block[
                    half * share : (half + 1) * share
                ]
        parts = [scratch[half, k ^ me] for k in range(scratch.shape[1])]
        rows_in_order = jnp.concatenate(parts, axis=0)
        out[...] = rows_in_order.astype(BF16)
        if half == 0:
            turned_ref[...] = rows_in_order.T.astype(BF16)


def weights_copies(sources, wanted, targets, sems):
    copies = []
    for i, ((which, start, width), target) in enumerate(zip(wanted, targets)):
        part = pl.ds(start, width)
        source = sources[which].at[part] if which == 2 else sources[which].at[:, part]
        copies.append(pltpu.make_async_copy(source, target, sems.at[i]))
    return copies


def fetch_kernel(wanted, me_ref, *refs):
    sources, targets, (done_ref, sems) = refs[:3], refs[3:-2], refs[-2:]
    copies = weights_copies(sources, wanted, targets, sems)
    for copy in copies:
        copy.start()
    done_ref[...] = jnp.zeros_like(done_ref)
    for copy in copies:
        copy.wait()


def forward_kernel(start, width, ready, wanted, own, sends, tile, tokens_ref, grads_ref, gate_ref, up_ref, *refs):
    if ready:
        down_ref, refs = refs[0], refs[1:]
    sources, refs = refs[:3], refs[4:]
    keep_ref, send_refs, refs = refs[0], refs[1 : 1 + sends], refs[1 + sends :]
    targets, refs = refs[: len(wanted)], refs[len(wanted) :]
    if not ready:
        down_ref, refs = refs[0], refs[1:]
        wanted, targets = ((2, start, width), *wanted), (down_ref, *targets)
    copies = weights_copies(sources, wanted, targets, refs[0])
    for copy in copies:
        copy.start()

    def put(i, at, part):
        to = pl.ds(pl.multiple_of(i * width + at, tile), tile)
        keep_ref[:, to] = part[:own]
        for s, ref in enumerate(send_refs):
            ref[:, to] = part[(s + 1) * own : (s + 2) * own].astype(BF16)

    @pl.loop(0, width // tile)
    def _(t):
        at = pl.multiple_of(t * tile, tile)
        put(0, at, jnp.dot(tokens_ref[...], gate_ref[:, pl.ds(at, tile)], preferred_element_type=F32))
        put(1, at, jnp.dot(tokens_ref[...], up_ref[:, pl.ds(at, tile)], preferred_element_type=F32))

    if not ready:
        copies[0].wait()

    @pl.loop(0, width // tile)
    def _(t):
        at = pl.multiple_of(t * tile, tile)
        down = down_ref[pl.ds(at, tile), :]
        put(2, at, lax.dot_general(grads_ref[...], down, CONTRACT_LAST, preferred_element_type=F32))

    for copy in copies[0 if ready else 1 :]:
        copy.wait()


def swiglu_kernel(width, n, after_ref, keep_ref, *refs):
    pieces, refs = refs[: n - 1], refs[n - 1 :]
    later, out_ref, send_refs = refs[: len(refs) // 2], refs[len(refs) // 2], refs[len(refs) // 2 + 1 :]
    sums = keep_ref[...]
    for ref in pieces:
        sums = sums + ref[:, : 3 * width].astype(F32)
    gate, upward, back = (sums[:, i * width : (i + 1) * width] for i in range(3))
    sigma = 1.0 / (1.0 + jnp.exp(-gate))
    parts = (back * upward * sigma * (1.0 + gate * (1.0 - sigma)), back * gate * sigma, gate * sigma * upward)
    for i, part in enumerate(parts):
        out_ref[:, i * width : (i + 1) * width] = part.astype(BF16)
    for before, after in zip(later, send_refs):
        split = before.shape[1]
        after[:, :split] = before[...]
        after[:, split:] = out_ref[...]


def input_kernel(width, n, me_ref, *refs):
    pieces, (gate_ref, up_ref, sum_ref, out_ref) = refs[:n], refs[n:]
    grads = jnp.concatenate([ref[:, : 2 * width] for ref in pieces], axis=0)
    own = pieces[0].shape[0]
    for at, size in tiles(gate_ref.shape[0], 512):
        rows = slice(at, at + size)
        part = lax.dot_general(grads[:, :width], gate_ref[rows, :], CONTRACT_LAST, preferred_element_type=F32)
        part += lax.dot_general(grads[:, width:], up_ref[rows, :], CONTRACT_LAST, preferred_element_type=F32)
        part += sum_ref[:, rows]
        for k in range(n):
            out_ref[pl.ds(pl.multiple_of((k ^ me_ref[0]) * own, 8), own), rows] = part[k * own : (k + 1) * own]


def backward_kernel(n, start, width, shift, begin, count, tile, n_in, adds, turned_ref, grads_ref, *refs):
    mine_ref, pieces, refs = refs[0], refs[1:n], refs[n:]
    bufs, sems = refs[-4:-1], refs[-1]
    outs, sum_refs = refs[n_in : n_in + 3], refs[n_in + 3 : -4]
    turned, grads = turned_ref[...], grads_ref[...]
    copies = []
    for t in range(count):
        slot, at = t % 2, begin + t * tile

        def rows(j):
            cols = j * width + at
            parts = [mine_ref[:, cols : cols + tile]] + [r[:, shift + cols : shift + cols + tile] for r in pieces]
            return jnp.concatenate(parts, axis=0)

        grad_gate, grad_up, hidden = rows(0), rows(1), rows(2)
        to = pl.ds(start + at, tile)
        if t >= 2:
            for copy in copies[t - 2]:
                copy.wait()
        targets = (outs[0].at[:, to], outs[1].at[:, to], outs[2].at[to])
        copies.append([pltpu.make_async_copy(b.at[slot], o, sems.at[slot, j]) for j, (b, o) in enumerate(zip(bufs, targets))])
        bufs[0][slot] = jnp.dot(turned, grad_gate, preferred_element_type=F32).astype(BF16)
        copies[t][0].start()
        bufs[1][slot] = jnp.dot(turned, grad_up, preferred_element_type=F32).astype(BF16)
        copies[t][1].start()
        bufs[2][slot] = lax.dot_general(hidden, grads, CONTRACT_FIRST, preferred_element_type=F32).astype(BF16)
        copies[t][2].start()
        for sum_ref in sum_refs:
            gate_ref, up_ref = refs[:2]
            part = lax.dot_general(grad_gate, gate_ref[:, at : at + tile], CONTRACT_LAST, preferred_element_type=F32)
            part += lax.dot_general(grad_up, up_ref[:, at : at + tile], CONTRACT_LAST, preferred_element_type=F32)
            if t > 0:
                part += sum_ref[...]
            elif adds:
                part += refs[2][...]
            sum_ref[...] = part
    for group in copies[-2:]:
        for copy in group:
            copy.wait()


def per_device(n_row, n_col, activations, out_grad, w_gate, w_up, w_down):
    share, depth = activations.shape
    hidden = w_gate.shape[1]
    total = share * n_col
    own = total // n_row
    me = lax.axis_index("row").astype(jnp.int32).reshape(1)
    w_gate, w_up, w_down = (pltpu.with_memory_space_constraint(w, pltpu.HBM) for w in (w_gate, w_up, w_down))
    unit = next(u for u in (512, 256, 128) if hidden % u == 0)
    small = max(unit // 2, 128)
    units = hidden // unit
    cuts = [0, 2 * units // 7 * unit, 4 * units // 7 * unit, hidden]
    one, two, three = ((a, b - a) for a, b in zip(cuts[:-1], cuts[1:]))

    def held(wanted):
        return [vmem((width, depth) if which == 2 else (depth, width), BF16) for which, _, width in wanted]

    mine = jnp.concatenate([activations, out_grad], axis=0)
    wanted = ((0, *one), (1, *one), (2, *one), (0, *two))
    gate_one, up_one, down_one, gate_two, fetched = pl.pallas_call(
        functools.partial(fetch_kernel, wanted),
        out_shape=held(wanted) + [shape((8, 128), F32)],
        in_specs=[SMEM] + [HBM] * 3,
        out_specs=[VMEM] * 5,
        scratch_shapes=[pltpu.SemaphoreType.DMA((4,))],
        compiler_params=PARAMS,
        name="fetch",
    )(me, w_gate, w_up, w_down)
    others = [exchange(mine, "col", n_col, 2 * k) for k in range(1, n_col // 2)]
    near = pl.pallas_call(
        join_kernel,
        out_shape=vmem((n_col * share, depth), BF16),
        in_specs=[VMEM] * (n_col // 2 + 1),
        out_specs=VMEM,
        compiler_params=PARAMS,
        name="join",
    )(mine, *others, fetched)
    far = exchange(near, "col", n_col, 1)
    tokens, grads, turned = pl.pallas_call(
        functools.partial(order_kernel, 2 * share),
        out_shape=[vmem((total, depth), BF16)] * 2 + [vmem((depth, total), BF16)],
        in_specs=[SMEM] + [VMEM] * 2,
        out_specs=[VMEM] * 3,
        scratch_shapes=[vmem((2, n_row, own, depth), F32)],
        compiler_params=PARAMS,
        name="order",
    )(me, near, far)

    def forward(start, width, gate, up, down, wanted, after):
        ready = down is not None
        keep, *rest = pl.pallas_call(
            functools.partial(forward_kernel, start, width, ready, wanted, own, n_row - 1, unit),
            out_shape=[vmem((own, 3 * width), F32)] + [vmem((own, 3 * width), BF16)] * (n_row - 1) + held(wanted),
            in_specs=[VMEM] * (5 if ready else 4) + [HBM] * 4,
            out_specs=[VMEM] * (n_row + len(wanted)),
            scratch_shapes=([] if ready else [vmem((width, depth), BF16)]) + [pltpu.SemaphoreType.DMA((3,))],
            compiler_params=PARAMS,
            name="forward",
        )(tokens, grads, gate, up, *([down] if ready else []), w_gate, w_up, w_down, after)
        return keep, rest[: n_row - 1], rest[n_row - 1 :]

    def to_others(blocks):
        return [exchange(x, "row", n_row, s + 1) for s, x in enumerate(blocks)]

    def swiglu(width, keep, got, later, after):
        mine, *sends = pl.pallas_call(
            functools.partial(swiglu_kernel, width, n_row),
            out_shape=[vmem((own, 3 * width), BF16)] + [vmem((own, x.shape[1] + 3 * width), BF16) for x in later],
            in_specs=[HBM] + [VMEM] * (n_row + len(later)),
            out_specs=[VMEM] * (1 + len(later)),
            compiler_params=PARAMS,
            name="swiglu",
        )(after, keep, *got, *later)
        return mine, sends

    def backward(start, width, shift, begin, count, tile, pieces, weights, outs, after, name):
        known = 2 + n_row + len(weights)
        return pl.pallas_call(
            functools.partial(
                backward_kernel, n_row, start, width, shift, begin, count // tile, tile,
                len(weights) + len(outs) + 1, len(weights) > 2,
            ),
            out_shape=[shape((depth, hidden), BF16)] * 2
            + [shape((hidden, depth), BF16)]
            + ([vmem((total, depth), F32)] if weights else []),
            in_specs=[VMEM] * known + [HBM] * (len(outs) + 1),
            out_specs=[HBM] * 3 + ([VMEM] if weights else []),
            input_output_aliases={known + k: k for k in range(len(outs))},
            scratch_shapes=[vmem((2, depth, tile), BF16)] * 2
            + [vmem((2, tile, depth), BF16), pltpu.SemaphoreType.DMA((2, 3))],
            compiler_params=PARAMS,
            name=name,
        )(turned, grads, *pieces, *weights, *outs, after)

    keep_one, sends, (up_two, gate_three) = forward(*one, gate_one, up_one, down_one, ((1, *two), (0, *three)), me)
    got_one = to_others(sends)
    keep_two, sends, (up_three,) = forward(*two, gate_two, up_two, None, ((1, *three),), me)
    mine_one, sends = swiglu(one[1], keep_one, got_one, sends, me)
    got_two = to_others(sends)
    keep_three, sends, _ = forward(*three, gate_three, up_three, None, (), mine_one)
    mine_two, sends = swiglu(two[1], keep_two, got_two, sends, me)
    got_three = to_others(sends)
    *outs, grad_input = backward(
        *one, 3 * two[1], 0, one[1], small, [mine_one, *got_two], (gate_one, up_one), (), mine_two, "backward_one"
    )
    mine_three, _ = swiglu(three[1], keep_three, got_three, (), grad_input)
    got_last = to_others([mine_three] * (n_row - 1))
    *outs, grad_input = backward(
        *two, 3 * three[1], 0, two[1], small, [mine_two, *got_three], (gate_two, up_two, grad_input), outs, mine_three, "backward_two"
    )
    pieces = [mine_three, *got_last]
    grad_input = pl.pallas_call(
        functools.partial(input_kernel, three[1], n_row),
        out_shape=vmem((total, depth), F32),
        in_specs=[SMEM] + [VMEM] * (n_row + 3),
        out_specs=VMEM,
        compiler_params=PARAMS,
        name="input_grad",
    )(me, *pieces, gate_three, up_three, grad_input)
    outs = backward(*three, 0, 0, unit, small, pieces, (), outs, me, "weight_grads_early")
    blocks = grad_input.reshape(n_col // 2, 2, share, depth)
    summed = blocks[:, 0] + exchange(blocks[:, 1], "col", n_col, 1)
    summed, *outs = lax.optimization_barrier((summed, *outs))
    outs = backward(*three, 0, unit, three[1] - unit, small, pieces, (), outs, me, "weight_grads")
    result = summed[0]
    for k in range(1, n_col // 2):
        result = result + exchange(summed[k], "col", n_col, 2 * k)
    return (result.astype(BF16), *outs)


def solution(mesh):
    in_specs = (P("col", "row"), P("col", "row"), P("row", "col"), P("row", "col"), P("col", "row"))
    out_specs = (P("col", "row"), P("row", "col"), P("row", "col"), P("col", "row"))
    return jax.shard_map(
        functools.partial(per_device, mesh.shape["row"], mesh.shape["col"]),
        mesh=mesh,
        in_specs=in_specs,
        out_specs=out_specs,
        check_vma=False,
    )
```

```python
import functools

import jax
import jax.numpy as jnp
from jax import lax
from jax.experimental import pallas as pl
from jax.experimental.pallas import tpu as pltpu
from jax.sharding import PartitionSpec as P

BF16, F32 = jnp.bfloat16, jnp.float32
HBM = pl.BlockSpec(memory_space=pl.ANY)
VMEM = pl.BlockSpec(memory_space=pltpu.VMEM)
SMEM = pl.BlockSpec(memory_space=pltpu.SMEM)
CONTRACT_LAST = (((1,), (1,)), ((), ()))
CONTRACT_FIRST = (((0,), (0,)), ((), ()))
CUTS = (0, 4, 12, 20, 28)
SPLIT = (0, 1, 2)
PARAMS = pltpu.CompilerParams(vmem_limit_bytes=14 << 20)
vmem = pltpu.VMEM
shape = jax.ShapeDtypeStruct


def exchange(x, axis, size, offset):
    return lax.ppermute(x, axis, [(i, i ^ offset) for i in range(size)])


def tile_of(width, most=512):
    return next(t for t in (512, 256, 128) if t <= most and width % t == 0)


def tiles(width, tile):
    return [(at, min(tile, width - at)) for at in range(0, width, tile)]


def pair_kernel(first_hbm, second_hbm, out_ref, both, sems):
    copies = [pltpu.make_async_copy(x, both.at[i], sems.at[i]) for i, x in enumerate((first_hbm, second_hbm))]
    for copy in copies:
        copy.start()
    for copy in copies:
        copy.wait()
    out_ref[...] = jnp.concatenate([both[0], both[1]], axis=0)


def join_kernel(*refs):
    rows = refs[0].shape[0]
    for i, ref in enumerate(refs[:-2]):
        refs[-1][i * rows : (i + 1) * rows, :] = ref[...]


def order_kernel(rows, me_ref, mine_ref, other_ref, tokens_ref, grads_ref, turned_ref, scratch):
    me = me_ref[0]
    share = rows // 2
    n = mine_ref.shape[0] // rows
    total = tokens_ref.shape[0]
    per_row = total // scratch.shape[1]
    for half, out in ((0, tokens_ref), (1, grads_ref)):
        for k in range(n):
            for c, ref in ((0, mine_ref), (1, other_ref)):
                block = ref[k * rows : (k + 1) * rows, :].astype(F32)
                at = (2 * k + c) * share
                scratch[half, at // per_row, at % per_row : at % per_row + share, :] = block[
                    half * share : (half + 1) * share
                ]
        parts = [scratch[half, k ^ me] for k in range(scratch.shape[1])]
        rows_in_order = jnp.concatenate(parts, axis=0)
        out[...] = rows_in_order.astype(BF16)
        if half == 0:
            turned_ref[...] = rows_in_order.T.astype(BF16)


def weights_copies(sources, wanted, targets, sems):
    copies = []
    for i, ((which, start, width), target) in enumerate(zip(wanted, targets)):
        part = pl.ds(start, width)
        source = sources[which].at[part] if which == 2 else sources[which].at[:, part]
        copies.append(pltpu.make_async_copy(source, target, sems.at[i]))
    return copies


def fetch_kernel(wanted, me_ref, *refs):
    sources, targets, (done_ref, sems) = refs[:3], refs[3:-2], refs[-2:]
    copies = weights_copies(sources, wanted, targets, sems)
    for copy in copies:
        copy.start()
    done_ref[...] = jnp.zeros_like(done_ref)
    for copy in copies:
        copy.wait()


def forward_kernel(start, width, ready, wanted, own, sends, tile, me_ref, tokens_ref, grads_ref, gate_ref, up_ref, *refs):
    if ready:
        down_ref, refs = refs[0], refs[1:]
    sources, refs = refs[:3], refs[4:]
    keep_ref, send_refs, refs = refs[0], refs[1 : 1 + sends], refs[1 + sends :]
    targets, refs = refs[: len(wanted)], refs[len(wanted) :]
    if not ready:
        down_ref, refs = refs[0], refs[1:]
        wanted, targets = ((2, start, width), *wanted), (down_ref, *targets)
    copies = weights_copies(sources, wanted, targets, refs[0])
    for copy in copies:
        copy.start()

    def put(i, at, part):
        to = slice(i * width + at, i * width + at + tile)
        keep_ref[:, to] = part[:own]
        for s, ref in enumerate(send_refs):
            ref[:, to] = part[(s + 1) * own : (s + 2) * own].astype(BF16)

    def gate_and_up():
        for at in range(0, width, tile):
            put(0, at, jnp.dot(tokens_ref[...], gate_ref[:, at : at + tile], preferred_element_type=F32))
            put(1, at, jnp.dot(tokens_ref[...], up_ref[:, at : at + tile], preferred_element_type=F32))

    def back():
        for at in range(0, width, tile):
            down = down_ref[at : at + tile, :]
            put(2, at, lax.dot_general(grads_ref[...], down, CONTRACT_LAST, preferred_element_type=F32))

    if ready:

        @pl.when(me_ref[0] >= 0)
        def _():
            gate_and_up()
            back()

        for copy in copies:
            copy.wait()
    else:
        pl.when(me_ref[0] >= 0)(gate_and_up)
        copies[0].wait()
        pl.when(me_ref[0] >= 0)(back)
        for copy in copies[1:]:
            copy.wait()


def swiglu_kernel(width, n, after_ref, keep_ref, *refs):
    pieces, refs = refs[: n - 1], refs[n - 1 :]
    later, out_ref, send_refs = refs[: len(refs) // 2], refs[len(refs) // 2], refs[len(refs) // 2 + 1 :]
    sums = keep_ref[...]
    for ref in pieces:
        sums = sums + ref[:, : 3 * width].astype(F32)
    gate, upward, back = (sums[:, i * width : (i + 1) * width] for i in range(3))
    sigma = 1.0 / (1.0 + jnp.exp(-gate))
    parts = (back * upward * sigma * (1.0 + gate * (1.0 - sigma)), back * gate * sigma, gate * sigma * upward)
    for i, part in enumerate(parts):
        out_ref[:, i * width : (i + 1) * width] = part.astype(BF16)
    for before, after in zip(later, send_refs):
        split = before.shape[1]
        after[:, :split] = before[...]
        after[:, split:] = out_ref[...]


def input_kernel(width, n, me_ref, *refs):
    pieces, (gate_ref, up_ref, sum_ref, out_ref) = refs[:n], refs[n:]
    grads = jnp.concatenate([ref[:, : 2 * width] for ref in pieces], axis=0)
    turned = (grads[:, :width].T, grads[:, width:].T)
    own = pieces[0].shape[0]
    for at, size in tiles(gate_ref.shape[0], 512):
        rows = slice(at, at + size)
        part = jnp.dot(gate_ref[rows, :], turned[0], preferred_element_type=F32)
        part += jnp.dot(up_ref[rows, :], turned[1], preferred_element_type=F32)
        part = (part + sum_ref[rows, :]).T
        for k in range(n):
            out_ref[pl.ds(pl.multiple_of((k ^ me_ref[0]) * own, 8), own), rows] = part[k * own : (k + 1) * own]


def backward_kernel(n, start, width, shift, begin, count, tile, n_in, adds, me_ref, turned_ref, grads_ref, *refs):
    mine_ref, pieces, refs = refs[0], refs[1:n], refs[n:]
    bufs, sems = refs[-4:-1], refs[-1]
    outs, sum_refs = refs[n_in : n_in + 3], refs[n_in + 3 : -4]

    def rows(j, at, size):
        cols = j * width + at
        parts = [mine_ref[:, cols : cols + size]] + [r[:, shift + cols : shift + cols + size] for r in pieces]
        return jnp.concatenate(parts, axis=0)

    def copies(t):
        to = pl.ds(start + begin + t * tile, tile)
        targets = (outs[0].at[:, to], outs[1].at[:, to], outs[2].at[to])
        return [pltpu.make_async_copy(b.at[t % 2], o, sems.at[t % 2, j]) for j, (b, o) in enumerate(zip(bufs, targets))]

    def products(t, which):
        at = begin + t * tile
        for j in which:
            if j == 2:
                part = lax.dot_general(rows(2, at, tile), grads_ref[...], CONTRACT_FIRST, preferred_element_type=F32)
            else:
                part = jnp.dot(turned_ref[...], rows(j, at, tile), preferred_element_type=F32)
            bufs[j][t % 2] = part.astype(BF16)
        into = copies(t)
        for j in which:
            into[j].start()

    for t in range(count):

        @pl.when(me_ref[0] >= 0)
        def _():
            if t >= 2:
                for copy in copies(t - 2):
                    copy.wait()
            products(t, SPLIT if t == 0 else (0, 1, 2))

        if t == 0:
            for j in range(len(SPLIT), 3):
                pl.when(me_ref[0] >= 0)(functools.partial(products, t, (j,)))

    for sum_ref in sum_refs:
        gate_ref, up_ref = refs[:2]
        cols = slice(begin, begin + count * tile)

        @pl.when(me_ref[0] >= 0)
        def _():
            part = jnp.dot(gate_ref[:, cols], rows(0, begin, count * tile).T, preferred_element_type=F32)
            part += jnp.dot(up_ref[:, cols], rows(1, begin, count * tile).T, preferred_element_type=F32)
            sum_ref[...] = part + refs[2][...] if adds else part

    for t in range(max(count - 2, 0), count):
        for copy in copies(t):
            copy.wait()


def per_device(n_row, n_col, activations, out_grad, w_gate, w_up, w_down):
    share, depth = activations.shape
    hidden = w_gate.shape[1]
    total = share * n_col
    own = total // n_row
    me = lax.axis_index("row").astype(jnp.int32).reshape(1)
    w_gate, w_up, w_down = (pltpu.with_memory_space_constraint(w, pltpu.HBM) for w in (w_gate, w_up, w_down))
    units = hidden // 128
    cuts = [-(-units * part // 28) * 128 for part in CUTS]
    chunks = [(a, b - a) for a, b in zip(cuts[:-1], cuts[1:])]
    one, two, three, four = chunks

    def held(wanted):
        return [vmem((width, depth) if which == 2 else (depth, width), BF16) for which, _, width in wanted]

    mine = pl.pallas_call(
        pair_kernel,
        out_shape=vmem((2 * share, depth), BF16),
        in_specs=[HBM] * 2,
        out_specs=VMEM,
        scratch_shapes=[vmem((2, share, depth), BF16), pltpu.SemaphoreType.DMA((2,))],
        compiler_params=PARAMS,
        name="pair",
    )(*(pltpu.with_memory_space_constraint(x, pltpu.HBM) for x in (activations, out_grad)))
    wanted = ((0, *one), (1, *one), (2, *one), (0, *two), (1, *two))
    gate_one, up_one, down_one, gate_two, up_two, fetched = pl.pallas_call(
        functools.partial(fetch_kernel, wanted),
        out_shape=held(wanted) + [shape((8, 128), F32)],
        in_specs=[SMEM] + [HBM] * 3,
        out_specs=[VMEM] * 6,
        scratch_shapes=[pltpu.SemaphoreType.DMA((5,))],
        compiler_params=PARAMS,
        name="fetch",
    )(me, w_gate, w_up, w_down)
    others = [exchange(mine, "col", n_col, 2 * k) for k in range(1, n_col // 2)]
    near = pl.pallas_call(
        join_kernel,
        out_shape=vmem((n_col * share, depth), BF16),
        in_specs=[VMEM] * (n_col // 2 + 1),
        out_specs=VMEM,
        compiler_params=PARAMS,
        name="join",
    )(mine, *others, fetched)
    far = exchange(near, "col", n_col, 1)
    tokens, grads, turned = pl.pallas_call(
        functools.partial(order_kernel, 2 * share),
        out_shape=[vmem((total, depth), BF16)] * 2 + [vmem((depth, total), BF16)],
        in_specs=[SMEM] + [VMEM] * 2,
        out_specs=[VMEM] * 3,
        scratch_shapes=[vmem((2, n_row, own, depth), F32)],
        compiler_params=PARAMS,
        name="order",
    )(me, near, far)

    def forward(start, width, gate, up, down, wanted, after):
        ready = down is not None
        keep, *rest = pl.pallas_call(
            functools.partial(forward_kernel, start, width, ready, wanted, own, n_row - 1, tile_of(width)),
            out_shape=[vmem((own, 3 * width), F32)] + [vmem((own, 3 * width), BF16)] * (n_row - 1) + held(wanted),
            in_specs=[SMEM] + [VMEM] * (5 if ready else 4) + [HBM] * 4,
            out_specs=[VMEM] * (n_row + len(wanted)),
            scratch_shapes=([] if ready else [vmem((width, depth), BF16)]) + [pltpu.SemaphoreType.DMA((3,))],
            compiler_params=PARAMS,
            name="forward",
        )(me, tokens, grads, gate, up, *([down] if ready else []), w_gate, w_up, w_down, after)
        return keep, rest[: n_row - 1], rest[n_row - 1 :]

    def to_others(blocks):
        return [exchange(x, "row", n_row, s + 1) for s, x in enumerate(blocks)]

    def swiglu(width, keep, got, later, after):
        mine, *sends = pl.pallas_call(
            functools.partial(swiglu_kernel, width, n_row),
            out_shape=[vmem((own, 3 * width), BF16)] + [vmem((own, x.shape[1] + 3 * width), BF16) for x in later],
            in_specs=[HBM] + [VMEM] * (n_row + len(later)),
            out_specs=[VMEM] * (1 + len(later)),
            compiler_params=PARAMS,
            name="swiglu",
        )(after, keep, *got, *later)
        return mine, sends

    def backward(start, width, shift, begin, count, tile, pieces, weights, outs, after, name):
        known = 3 + n_row + len(weights)
        return pl.pallas_call(
            functools.partial(
                backward_kernel, n_row, start, width, shift, begin, count // tile, tile,
                len(weights) + len(outs) + 1, len(weights) > 2,
            ),
            out_shape=[shape((depth, hidden), BF16)] * 2
            + [shape((hidden, depth), BF16)]
            + ([vmem((depth, total), F32)] if weights else []),
            in_specs=[SMEM] + [VMEM] * (known - 1) + [HBM] * (len(outs) + 1),
            out_specs=[HBM] * 3 + ([VMEM] if weights else []),
            input_output_aliases={known + k: k for k in range(len(outs))},
            scratch_shapes=[vmem((2, depth, tile), BF16)] * 2
            + [vmem((2, tile, depth), BF16), pltpu.SemaphoreType.DMA((2, 3))],
            compiler_params=PARAMS,
            name=name,
        )(me, turned, grads, *pieces, *weights, *outs, after)

    keep_one, sends, (down_two,) = forward(*one, gate_one, up_one, down_one, ((2, *two),), me)
    got_one = to_others(sends)
    keep_two, sends, (gate_three, up_three) = forward(*two, gate_two, up_two, down_two, ((0, *three), (1, *three)), me)
    mine_one, sends = swiglu(one[1], keep_one, got_one, sends, me)
    got_two = to_others(sends)
    keep_three, sends, (gate_four, up_four) = forward(*three, gate_three, up_three, None, ((0, *four), (1, *four)), mine_one)
    mine_two, sends = swiglu(two[1], keep_two, got_two, sends, me)
    got_three = to_others(sends)
    keep_four, sends, _ = forward(*four, gate_four, up_four, None, (), mine_two)
    *outs, grad_input = backward(
        *one, 3 * two[1], 0, one[1], tile_of(one[1], 256), [mine_one, *got_two], (gate_one, up_one), (), mine_two, "backward_one"
    )
    mine_three, sends = swiglu(three[1], keep_three, got_three, sends, grad_input)
    got_four = to_others(sends)
    *outs, grad_input = backward(
        *two, 3 * three[1], 0, two[1], tile_of(two[1]), [mine_two, *got_three], (gate_two, up_two, grad_input), outs, mine_three, "backward_two"
    )
    mine_four, _ = swiglu(four[1], keep_four, got_four, (), grad_input)
    got_last = to_others([mine_four] * (n_row - 1))
    *outs, grad_input = backward(
        *three, 3 * four[1], 0, three[1], tile_of(three[1]), [mine_three, *got_four], (gate_three, up_three, grad_input), outs, mine_four, "backward_three"
    )
    pieces = [mine_four, *got_last]
    grad_input = pl.pallas_call(
        functools.partial(input_kernel, four[1], n_row),
        out_shape=vmem((total, depth), F32),
        in_specs=[SMEM] + [VMEM] * (n_row + 3),
        out_specs=VMEM,
        compiler_params=PARAMS,
        name="input_grad",
    )(me, *pieces, gate_four, up_four, grad_input)
    blocks = grad_input.reshape(n_col // 2, 2, share, depth)
    summed = blocks[:, 0] + exchange(blocks[:, 1], "col", n_col, 1)
    outs = backward(*four, 0, 0, four[1], tile_of(four[1], 256), pieces, (), outs, summed, "weight_grads")
    result = summed[0]
    for k in range(1, n_col // 2):
        result = result + exchange(summed[k], "col", n_col, 2 * k)
    return (result.astype(BF16), *outs)


def solution(mesh):
    in_specs = (P("col", "row"), P("col", "row"), P("row", "col"), P("row", "col"), P("col", "row"))
    out_specs = (P("col", "row"), P("row", "col"), P("row", "col"), P("col", "row"))
    return jax.shard_map(
        functools.partial(per_device, mesh.shape["row"], mesh.shape["col"]),
        mesh=mesh,
        in_specs=in_specs,
        out_specs=out_specs,
        check_vma=False,
    )
```

```python
import functools

import jax
import jax.numpy as jnp
from jax import lax
from jax.experimental import pallas as pl
from jax.experimental.pallas import tpu as pltpu
from jax.sharding import PartitionSpec as P

BF16, F32 = jnp.bfloat16, jnp.float32
HBM = pl.BlockSpec(memory_space=pl.ANY)
VMEM = pl.BlockSpec(memory_space=pltpu.VMEM)
SMEM = pl.BlockSpec(memory_space=pltpu.SMEM)
CONTRACT_LAST = (((1,), (1,)), ((), ()))
CONTRACT_FIRST = (((0,), (0,)), ((), ()))
CUTS = (0, 8, 16, 26, 28)
SPLIT = (0, 1, 2)
PARAMS = pltpu.CompilerParams(vmem_limit_bytes=15 << 20)
vmem = pltpu.VMEM
shape = jax.ShapeDtypeStruct


def exchange(x, axis, size, offset):
    return lax.ppermute(x, axis, [(i, i ^ offset) for i in range(size)])


def tile_of(width, most=512):
    return next(t for t in (512, 256, 128) if t <= most and width % t == 0)


def tiles(width, tile):
    return [(at, min(tile, width - at)) for at in range(0, width, tile)]


def pair_kernel(first_hbm, second_hbm, out_ref, both, sems):
    copies = [pltpu.make_async_copy(x, both.at[i], sems.at[i]) for i, x in enumerate((first_hbm, second_hbm))]
    for copy in copies:
        copy.start()
    for copy in copies:
        copy.wait()
    out_ref[...] = jnp.concatenate([both[0], both[1]], axis=0)


def join_kernel(*refs):
    rows = refs[0].shape[0]
    for i, ref in enumerate(refs[:-2]):
        refs[-1][i * rows : (i + 1) * rows, :] = ref[...]


def order_kernel(rows, me_ref, mine_ref, other_ref, tokens_ref, grads_ref, turned_ref, scratch):
    me = me_ref[0]
    share = rows // 2
    n = mine_ref.shape[0] // rows
    total = tokens_ref.shape[0]
    per_row = total // scratch.shape[1]
    for half, out in ((0, tokens_ref), (1, grads_ref)):
        for k in range(n):
            for c, ref in ((0, mine_ref), (1, other_ref)):
                block = ref[k * rows : (k + 1) * rows, :].astype(F32)
                at = (2 * k + c) * share
                scratch[half, at // per_row, at % per_row : at % per_row + share, :] = block[
                    half * share : (half + 1) * share
                ]
        parts = [scratch[half, k ^ me] for k in range(scratch.shape[1])]
        rows_in_order = jnp.concatenate(parts, axis=0)
        out[...] = rows_in_order.astype(BF16)
        if half == 0:
            turned_ref[...] = rows_in_order.T.astype(BF16)


def weights_copies(sources, wanted, targets, sems):
    copies = []
    for i, ((which, start, width), target) in enumerate(zip(wanted, targets)):
        part = pl.ds(start, width)
        source = sources[which].at[part] if which == 2 else sources[which].at[:, part]
        copies.append(pltpu.make_async_copy(source, target, sems.at[i]))
    return copies


def fetch_kernel(wanted, me_ref, *refs):
    sources, targets, (done_ref, sems) = refs[:3], refs[3:-2], refs[-2:]
    copies = weights_copies(sources, wanted, targets, sems)
    for copy in copies:
        copy.start()
    done_ref[...] = jnp.zeros_like(done_ref)
    for copy in copies:
        copy.wait()


def forward_kernel(start, width, given, wanted, own, sends, tile, me_ref, tokens_ref, grads_ref, *refs):
    weights, refs = dict(zip(given, refs)), refs[len(given) :]
    sources, refs = refs[:3], refs[4:]
    keep_ref, send_refs, refs = refs[0], refs[1 : 1 + max(sends, 1)], refs[1 + max(sends, 1) :]
    send_ref = send_refs[0]
    targets, refs = refs[: len(wanted)], refs[len(wanted) :]
    streamed = [which for which in (0, 2, 1) if which not in given]
    if 2 in streamed:
        wanted, targets = ((2, start, width), *wanted), (refs[0], *targets)
    pairs = sorted(zip(wanted, targets), key=lambda p: streamed.index(p[0][0]) if p[0] == (p[0][0], start, width) else 3)
    copies = weights_copies(sources, [p[0] for p in pairs], [p[1] for p in pairs], refs[-1])
    for copy in copies:
        copy.start()
    for which, (_, target) in zip(streamed, pairs):
        weights[which] = target

    def put(i, at, part):
        to = i * width + at
        if sends == 0:
            keep_ref[:, to : to + tile] = part
            for k in range(part.shape[0] // own):
                send_ref[:, 3 * k * width + to : 3 * k * width + to + tile] = part[k * own : (k + 1) * own].astype(BF16)
        else:
            keep_ref[:, to : to + tile] = part[:own]
            for s, ref in enumerate(send_refs):
                ref[:, to : to + tile] = part[(s + 1) * own : (s + 2) * own].astype(BF16)

    def product(which):
        for at in range(0, width, tile):
            if which == 2:
                down = weights[2][at : at + tile, :]
                put(2, at, lax.dot_general(grads_ref[...], down, CONTRACT_LAST, preferred_element_type=F32))
            else:
                columns = weights[which][:, at : at + tile]
                put(which, at, jnp.dot(tokens_ref[...], columns, preferred_element_type=F32))

    if given:

        @pl.when(me_ref[0] >= 0)
        def _():
            for which in given:
                product(which)

    for which, copy in zip(streamed, copies):
        copy.wait()
        pl.when(me_ref[0] >= 0)(functools.partial(product, which))
    for copy in copies[len(streamed) :]:
        copy.wait()


def gradients(sums, width):
    gate, upward, back = (sums[:, i * width : (i + 1) * width] for i in range(3))
    sigma = 1.0 / (1.0 + jnp.exp(-gate))
    return back * upward * sigma * (1.0 + gate * (1.0 - sigma)), back * gate * sigma, gate * sigma * upward


def swiglu_kernel(width, n, after_ref, keep_ref, *refs):
    pieces, refs = refs[: n - 1], refs[n - 1 :]
    later, out_ref, send_refs = refs[: len(refs) // 2], refs[len(refs) // 2], refs[len(refs) // 2 + 1 :]
    sums = keep_ref[...]
    for ref in pieces:
        sums = sums + ref[:, : 3 * width].astype(F32)
    for i, part in enumerate(gradients(sums, width)):
        out_ref[:, i * width : (i + 1) * width] = part.astype(BF16)
    for before, after in zip(later, send_refs):
        split = before.shape[1]
        after[:, :split] = before[...]
        after[:, split:] = out_ref[...]


def swiglu_all_kernel(width, n, after_ref, keep_ref, *refs):
    pieces, out_refs = refs[: n - 1], refs[n - 1 :]
    own = out_refs[0].shape[0]
    for k, out_ref in enumerate(out_refs):
        sums = keep_ref[k * own : (k + 1) * own, :]
        for s, ref in enumerate(pieces):
            at = 3 * (k ^ (s + 1)) * width
            sums = sums + ref[:, at : at + 3 * width].astype(F32)
        for i, part in enumerate(gradients(sums, width)):
            out_ref[:, i * width : (i + 1) * width] = part.astype(BF16)


def input_kernel(n, chunks, me_ref, *refs):
    sum_ref, out_ref = refs[-2:]
    products = []
    for i, (width, shift) in enumerate(chunks):
        mine_ref, *pieces = refs[i * n : (i + 1) * n]
        weights = refs[n * len(chunks) + 2 * i : n * len(chunks) + 2 * i + 2]
        for j, ref in enumerate(weights):
            cols = slice(j * width, (j + 1) * width)
            others = [r[:, shift + j * width : shift + (j + 1) * width] for r in pieces]
            products.append((ref, jnp.concatenate([mine_ref[:, cols]] + others, axis=0).T))
    own = refs[0].shape[0]
    for at, size in tiles(sum_ref.shape[0], 512):
        rows = slice(at, at + size)
        part = sum_ref[rows, :]
        for ref, grads in products:
            part += jnp.dot(ref[rows, :], grads, preferred_element_type=F32)
        part = part.T
        for k in range(n):
            out_ref[pl.ds(pl.multiple_of((k ^ me_ref[0]) * own, 8), own), rows] = part[k * own : (k + 1) * own]


def backward_kernel(n, start, width, shift, begin, count, tile, n_in, adds, me_ref, turned_ref, grads_ref, *refs):
    mine_ref, pieces, refs = refs[0], refs[1:n], refs[n:]
    bufs, sems = refs[-4:-1], refs[-1]
    outs, sum_refs = refs[n_in : n_in + 3], refs[n_in + 3 : -4]

    def rows(j, at, size):
        cols = j * width + at
        parts = [mine_ref[:, cols : cols + size]] + [r[:, shift + cols : shift + cols + size] for r in pieces]
        return jnp.concatenate(parts, axis=0)

    def copies(t):
        to = pl.ds(start + begin + t * tile, tile)
        targets = (outs[0].at[:, to], outs[1].at[:, to], outs[2].at[to])
        return [pltpu.make_async_copy(b.at[t % 2], o, sems.at[t % 2, j]) for j, (b, o) in enumerate(zip(bufs, targets))]

    def products(t, which):
        at = begin + t * tile
        for j in which:
            if j == 2:
                part = lax.dot_general(rows(2, at, tile), grads_ref[...], CONTRACT_FIRST, preferred_element_type=F32)
            else:
                part = jnp.dot(turned_ref[...], rows(j, at, tile), preferred_element_type=F32)
            bufs[j][t % 2] = part.astype(BF16)
        into = copies(t)
        for j in which:
            into[j].start()

    for t in range(count):

        @pl.when(me_ref[0] >= 0)
        def _():
            if t >= 2:
                for copy in copies(t - 2):
                    copy.wait()
            products(t, SPLIT if t == 0 else (0, 1, 2))

        if t == 0:
            for j in range(len(SPLIT), 3):
                pl.when(me_ref[0] >= 0)(functools.partial(products, t, (j,)))

    for sum_ref in sum_refs:
        gate_ref, up_ref = refs[:2]
        cols = slice(begin, begin + count * tile)

        @pl.when(me_ref[0] >= 0)
        def _():
            part = jnp.dot(gate_ref[:, cols], rows(0, begin, count * tile).T, preferred_element_type=F32)
            part += jnp.dot(up_ref[:, cols], rows(1, begin, count * tile).T, preferred_element_type=F32)
            sum_ref[...] = part + refs[2][...] if adds else part

    for t in range(max(count - 2, 0), count):
        for copy in copies(t):
            copy.wait()


def per_device(n_row, n_col, activations, out_grad, w_gate, w_up, w_down):
    share, depth = activations.shape
    hidden = w_gate.shape[1]
    total = share * n_col
    own = total // n_row
    me = lax.axis_index("row").astype(jnp.int32).reshape(1)
    w_gate, w_up, w_down = (pltpu.with_memory_space_constraint(w, pltpu.HBM) for w in (w_gate, w_up, w_down))
    units = hidden // 128
    cuts = [128 * min(-(-units * part // 28), units - (len(CUTS) - 1 - i)) for i, part in enumerate(CUTS)]
    one, two, three, four = ((a, b - a) for a, b in zip(cuts[:-1], cuts[1:]))

    def held(wanted):
        return [vmem((width, depth) if which == 2 else (depth, width), BF16) for which, _, width in wanted]

    mine = pl.pallas_call(
        pair_kernel,
        out_shape=vmem((2 * share, depth), BF16),
        in_specs=[HBM] * 2,
        out_specs=VMEM,
        scratch_shapes=[vmem((2, share, depth), BF16), pltpu.SemaphoreType.DMA((2,))],
        compiler_params=PARAMS,
        name="pair",
    )(*(pltpu.with_memory_space_constraint(x, pltpu.HBM) for x in (activations, out_grad)))
    wanted = ((0, *one), (1, *one), (2, *one))
    gate_one, up_one, down_one, fetched = pl.pallas_call(
        functools.partial(fetch_kernel, wanted),
        out_shape=held(wanted) + [shape((8, 128), F32)],
        in_specs=[SMEM] + [HBM] * 3,
        out_specs=[VMEM] * 4,
        scratch_shapes=[pltpu.SemaphoreType.DMA((3,))],
        compiler_params=PARAMS,
        name="fetch",
    )(me, w_gate, w_up, w_down)
    others = [exchange(mine, "col", n_col, 2 * k) for k in range(1, n_col // 2)]
    near = pl.pallas_call(
        join_kernel,
        out_shape=vmem((n_col * share, depth), BF16),
        in_specs=[VMEM] * (n_col // 2 + 1),
        out_specs=VMEM,
        compiler_params=PARAMS,
        name="join",
    )(mine, *others, fetched)
    far = exchange(near, "col", n_col, 1)
    tokens, grads, turned = pl.pallas_call(
        functools.partial(order_kernel, 2 * share),
        out_shape=[vmem((total, depth), BF16)] * 2 + [vmem((depth, total), BF16)],
        in_specs=[SMEM] + [VMEM] * 2,
        out_specs=[VMEM] * 3,
        scratch_shapes=[vmem((2, n_row, own, depth), F32)],
        compiler_params=PARAMS,
        name="order",
    )(me, near, far)

    def forward(start, width, gate, up, down, wanted, after, whole=False):
        weights = (gate, up, down)
        given = tuple(i for i, x in enumerate(weights) if x is not None)
        sends = 0 if whole else n_row - 1
        if whole:
            sums = [vmem((total, 3 * width), F32), vmem((own, 3 * n_row * width), BF16)]
        else:
            sums = [vmem((own, 3 * width), F32)] + [vmem((own, 3 * width), BF16)] * sends
        keep, *rest = pl.pallas_call(
            functools.partial(forward_kernel, start, width, given, wanted, own, sends, tile_of(width)),
            out_shape=sums + held(wanted),
            in_specs=[SMEM] + [VMEM] * (2 + len(given)) + [HBM] * 4,
            out_specs=[VMEM] * (len(sums) + len(wanted)),
            scratch_shapes=([vmem((width, depth), BF16)] if down is None else []) + [pltpu.SemaphoreType.DMA((len(wanted) + 1,))],
            compiler_params=PARAMS,
            name="forward",
        )(me, tokens, grads, *(x for x in weights if x is not None), w_gate, w_up, w_down, after)
        return keep, rest[: len(sums) - 1], rest[len(sums) - 1 :]

    def to_others(blocks):
        return [exchange(x, "row", n_row, s + 1) for s, x in enumerate(blocks)]

    def swiglu(width, keep, got, later, after):
        mine, *sends = pl.pallas_call(
            functools.partial(swiglu_kernel, width, n_row),
            out_shape=[vmem((own, 3 * width), BF16)] + [vmem((own, x.shape[1] + 3 * width), BF16) for x in later],
            in_specs=[HBM] + [VMEM] * (n_row + len(later)),
            out_specs=[VMEM] * (1 + len(later)),
            compiler_params=PARAMS,
            name="swiglu",
        )(after, keep, *got, *later)
        return mine, sends

    def backward(start, width, shift, begin, count, tile, pieces, weights, outs, after, name):
        known = 3 + n_row + len(weights)
        return pl.pallas_call(
            functools.partial(
                backward_kernel, n_row, start, width, shift, begin, count // tile, tile,
                len(weights) + len(outs) + 1, len(weights) > 2,
            ),
            out_shape=[shape((depth, hidden), BF16)] * 2
            + [shape((hidden, depth), BF16)]
            + ([vmem((depth, total), F32)] if weights else []),
            in_specs=[SMEM] + [VMEM] * (known - 1) + [HBM] * (len(outs) + 1),
            out_specs=[HBM] * 3 + ([VMEM] if weights else []),
            input_output_aliases={known + k: k for k in range(len(outs))},
            scratch_shapes=[vmem((2, depth, tile), BF16)] * 2
            + [vmem((2, tile, depth), BF16), pltpu.SemaphoreType.DMA((2, 3))],
            compiler_params=PARAMS,
            name=name,
        )(me, turned, grads, *pieces, *weights, *outs, after)

    keep_one, sends, (gate_two,) = forward(*one, gate_one, up_one, down_one, ((0, *two),), me)
    got_one = to_others(sends)
    keep_two, sends, (up_two,) = forward(*two, gate_two, None, None, ((1, *two),), me)
    mine_one, sends = swiglu(one[1], keep_one, got_one, sends, me)
    got_two = to_others(sends)
    keep_three, sends, (gate_three, up_three, gate_four, up_four, down_four) = forward(
        *three, None, None, None, ((0, *three), (1, *three), (0, *four), (1, *four), (2, *four)), mine_one
    )
    mine_two, sends = swiglu(two[1], keep_two, got_two, sends, me)
    got_three = to_others(sends)
    keep_four, sends, _ = forward(*four, gate_four, up_four, down_four, (), mine_two, whole=True)
    *outs, grad_input = backward(
        *one, 3 * two[1], 0, one[1], tile_of(one[1]), [mine_one, *got_two], (gate_one, up_one), (), mine_two, "backward_one"
    )
    mine_three, sends = swiglu(three[1], keep_three, got_three, sends, grad_input)
    got_four = to_others(sends * (n_row - 1))
    *outs, grad_input = backward(
        *two, 3 * three[1], 0, two[1], tile_of(two[1]), [mine_two, *got_three], (gate_two, up_two, grad_input), outs, mine_three, "backward_two"
    )
    pieces = [mine_three, *got_four]
    pieces_four = pl.pallas_call(
        functools.partial(swiglu_all_kernel, four[1], n_row),
        out_shape=[vmem((own, 3 * four[1]), BF16)] * n_row,
        in_specs=[HBM] + [VMEM] * n_row,
        out_specs=[VMEM] * n_row,
        compiler_params=PARAMS,
        name="swiglu_all",
    )(grad_input, keep_four, *got_four)
    shift = 3 * n_row * four[1]
    grad_input = pl.pallas_call(
        functools.partial(input_kernel, n_row, ((three[1], shift), (four[1], 0))),
        out_shape=vmem((total, depth), F32),
        in_specs=[SMEM] + [VMEM] * (2 * n_row + 5),
        out_specs=VMEM,
        compiler_params=PARAMS,
        name="input_grad",
    )(me, *pieces, *pieces_four, gate_three, up_three, gate_four, up_four, grad_input)
    blocks = grad_input.reshape(n_col // 2, 2, share, depth)
    outs = backward(*four, 0, 0, four[1], tile_of(four[1], 256), pieces_four, (), outs, grad_input, "weight_grads_early")
    other = exchange(blocks[:, 1], "col", n_col, 1)
    other, *outs = lax.optimization_barrier((other, *outs))
    summed = blocks[:, 0] + other
    outs = backward(*three, shift, 0, three[1], tile_of(three[1], 256), pieces, (), outs, summed, "weight_grads")
    result = summed[0]
    for k in range(1, n_col // 2):
        result = result + exchange(summed[k], "col", n_col, 2 * k)
    return (result.astype(BF16), *outs)


def solution(mesh):
    in_specs = (P("col", "row"), P("col", "row"), P("row", "col"), P("row", "col"), P("col", "row"))
    out_specs = (P("col", "row"), P("row", "col"), P("row", "col"), P("col", "row"))
    return jax.shard_map(
        functools.partial(per_device, mesh.shape["row"], mesh.shape["col"]),
        mesh=mesh,
        in_specs=in_specs,
        out_specs=out_specs,
        check_vma=False,
    )
```

```python
import functools

import jax
import jax.numpy as jnp
from jax import lax
from jax.experimental import pallas as pl
from jax.experimental.pallas import tpu as pltpu
from jax.sharding import PartitionSpec as P

BF16, F32 = jnp.bfloat16, jnp.float32
HBM = pl.BlockSpec(memory_space=pl.ANY)
VMEM = pl.BlockSpec(memory_space=pltpu.VMEM)
SMEM = pl.BlockSpec(memory_space=pltpu.SMEM)
CONTRACT_LAST = (((1,), (1,)), ((), ()))
CONTRACT_FIRST = (((0,), (0,)), ((), ()))
CUTS = (0, 8, 16, 26, 28)
SPLIT = (0, 1, 2)
PARAMS = pltpu.CompilerParams(vmem_limit_bytes=15 << 20)
vmem = pltpu.VMEM
shape = jax.ShapeDtypeStruct


def exchange(x, axis, size, offset):
    return lax.ppermute(x, axis, [(i, i ^ offset) for i in range(size)])


def tile_of(width, most=512):
    return next(t for t in (512, 256, 128) if t <= most and width % t == 0)


def tiles(width, tile):
    return [(at, min(tile, width - at)) for at in range(0, width, tile)]


def pair_kernel(first_hbm, second_hbm, out_ref, both, sems):
    copies = [pltpu.make_async_copy(x, both.at[i], sems.at[i]) for i, x in enumerate((first_hbm, second_hbm))]
    for copy in copies:
        copy.start()
    for copy in copies:
        copy.wait()
    out_ref[...] = jnp.concatenate([both[0], both[1]], axis=0)


def join_kernel(*refs):
    rows = refs[0].shape[0]
    for i, ref in enumerate(refs[:-2]):
        refs[-1][i * rows : (i + 1) * rows, :] = ref[...]


def order_kernel(rows, me_ref, mine_ref, other_ref, tokens_ref, grads_ref, scratch):
    me = me_ref[0]
    share = rows // 2
    n = mine_ref.shape[0] // rows
    total = tokens_ref.shape[0]
    per_row = total // scratch.shape[1]
    for half, out in ((0, tokens_ref), (1, grads_ref)):
        for k in range(n):
            for c, ref in ((0, mine_ref), (1, other_ref)):
                block = ref[k * rows : (k + 1) * rows, :].astype(F32)
                at = (2 * k + c) * share
                scratch[half, at // per_row, at % per_row : at % per_row + share, :] = block[
                    half * share : (half + 1) * share
                ]
        parts = [scratch[half, k ^ me] for k in range(scratch.shape[1])]
        out[...] = jnp.concatenate(parts, axis=0).astype(BF16)


def turn_kernel(tokens_ref, after_ref, turned_ref):
    turned_ref[...] = tokens_ref[...].astype(F32).T.astype(BF16)


def weights_copies(sources, wanted, targets, sems):
    copies = []
    for i, ((which, start, width), target) in enumerate(zip(wanted, targets)):
        part = pl.ds(start, width)
        source = sources[which].at[part] if which == 2 else sources[which].at[:, part]
        copies.append(pltpu.make_async_copy(source, target, sems.at[i]))
    return copies


def fetch_kernel(wanted, me_ref, *refs):
    sources, targets, (done_ref, sems) = refs[:3], refs[3:-2], refs[-2:]
    copies = weights_copies(sources, wanted, targets, sems)
    for copy in copies:
        copy.start()
    done_ref[...] = jnp.zeros_like(done_ref)
    for copy in copies:
        copy.wait()


def forward_kernel(start, width, given, wanted, own, sends, tile, me_ref, tokens_ref, grads_ref, *refs):
    weights, refs = dict(zip(given, refs)), refs[len(given) :]
    sources, refs = refs[:3], refs[4:]
    keep_ref, send_refs, refs = refs[0], refs[1 : 1 + max(sends, 1)], refs[1 + max(sends, 1) :]
    send_ref = send_refs[0]
    targets, refs = refs[: len(wanted)], refs[len(wanted) :]
    streamed = [which for which in (0, 2, 1) if which not in given]
    if 2 in streamed:
        wanted, targets = ((2, start, width), *wanted), (refs[0], *targets)
    pairs = sorted(zip(wanted, targets), key=lambda p: streamed.index(p[0][0]) if p[0] == (p[0][0], start, width) else 3)
    copies = weights_copies(sources, [p[0] for p in pairs], [p[1] for p in pairs], refs[-1])
    for copy in copies:
        copy.start()
    for which, (_, target) in zip(streamed, pairs):
        weights[which] = target

    def put(i, at, part):
        to = i * width + at
        if sends == 0:
            keep_ref[:, to : to + tile] = part
            for k in range(part.shape[0] // own):
                send_ref[:, 3 * k * width + to : 3 * k * width + to + tile] = part[k * own : (k + 1) * own].astype(BF16)
        else:
            keep_ref[:, to : to + tile] = part[:own]
            for s, ref in enumerate(send_refs):
                ref[:, to : to + tile] = part[(s + 1) * own : (s + 2) * own].astype(BF16)

    def product(which):
        for at in range(0, width, tile):
            if which == 2:
                down = weights[2][at : at + tile, :]
                put(2, at, lax.dot_general(grads_ref[...], down, CONTRACT_LAST, preferred_element_type=F32))
            else:
                columns = weights[which][:, at : at + tile]
                put(which, at, jnp.dot(tokens_ref[...], columns, preferred_element_type=F32))

    if given:

        @pl.when(me_ref[0] >= 0)
        def _():
            for which in given:
                product(which)

    for which, copy in zip(streamed, copies):
        copy.wait()
        pl.when(me_ref[0] >= 0)(functools.partial(product, which))
    for copy in copies[len(streamed) :]:
        copy.wait()


def gradients(sums, width):
    gate, upward, back = (sums[:, i * width : (i + 1) * width] for i in range(3))
    sigma = 1.0 / (1.0 + jnp.exp(-gate))
    return back * upward * sigma * (1.0 + gate * (1.0 - sigma)), back * gate * sigma, gate * sigma * upward


def swiglu_kernel(width, n, after_ref, keep_ref, *refs):
    pieces, refs = refs[: n - 1], refs[n - 1 :]
    later, out_ref, send_refs = refs[: len(refs) // 2], refs[len(refs) // 2], refs[len(refs) // 2 + 1 :]
    sums = keep_ref[...]
    for ref in pieces:
        sums = sums + ref[:, : 3 * width].astype(F32)
    for i, part in enumerate(gradients(sums, width)):
        out_ref[:, i * width : (i + 1) * width] = part.astype(BF16)
    for before, after in zip(later, send_refs):
        split = before.shape[1]
        after[:, :split] = before[...]
        after[:, split:] = out_ref[...]


def swiglu_all_kernel(width, n, after_ref, keep_ref, *refs):
    pieces, out_refs = refs[: n - 1], refs[n - 1 :]
    own = out_refs[0].shape[0]
    for k, out_ref in enumerate(out_refs):
        sums = keep_ref[k * own : (k + 1) * own, :]
        for s, ref in enumerate(pieces):
            at = 3 * (k ^ (s + 1)) * width
            sums = sums + ref[:, at : at + 3 * width].astype(F32)
        for i, part in enumerate(gradients(sums, width)):
            out_ref[:, i * width : (i + 1) * width] = part.astype(BF16)


def input_kernel(n, chunks, me_ref, *refs):
    sum_ref, out_ref = refs[-2:]
    products = []
    for i, (width, shift) in enumerate(chunks):
        mine_ref, *pieces = refs[i * n : (i + 1) * n]
        weights = refs[n * len(chunks) + 2 * i : n * len(chunks) + 2 * i + 2]
        for j, ref in enumerate(weights):
            cols = slice(j * width, (j + 1) * width)
            others = [r[:, shift + j * width : shift + (j + 1) * width] for r in pieces]
            products.append((ref, jnp.concatenate([mine_ref[:, cols]] + others, axis=0).T))
    own = refs[0].shape[0]
    for at, size in tiles(sum_ref.shape[0], 512):
        rows = slice(at, at + size)
        part = sum_ref[rows, :]
        for ref, grads in products:
            part += jnp.dot(ref[rows, :], grads, preferred_element_type=F32)
        part = part.T
        for k in range(n):
            out_ref[pl.ds(pl.multiple_of((k ^ me_ref[0]) * own, 8), own), rows] = part[k * own : (k + 1) * own]


def backward_kernel(n, start, width, shift, begin, count, tile, n_in, adds, me_ref, turned_ref, grads_ref, *refs):
    mine_ref, pieces, refs = refs[0], refs[1:n], refs[n:]
    bufs, sems = refs[-4:-1], refs[-1]
    outs, sum_refs = refs[n_in : n_in + 3], refs[n_in + 3 : -4]

    def rows(j, at, size):
        cols = j * width + at
        parts = [mine_ref[:, cols : cols + size]] + [r[:, shift + cols : shift + cols + size] for r in pieces]
        return jnp.concatenate(parts, axis=0)

    def copies(t):
        to = pl.ds(start + begin + t * tile, tile)
        targets = (outs[0].at[:, to], outs[1].at[:, to], outs[2].at[to])
        return [pltpu.make_async_copy(b.at[t % 2], o, sems.at[t % 2, j]) for j, (b, o) in enumerate(zip(bufs, targets))]

    def products(t, which):
        at = begin + t * tile
        for j in which:
            if j == 2:
                part = lax.dot_general(rows(2, at, tile), grads_ref[...], CONTRACT_FIRST, preferred_element_type=F32)
            else:
                part = jnp.dot(turned_ref[...], rows(j, at, tile), preferred_element_type=F32)
            bufs[j][t % 2] = part.astype(BF16)
        into = copies(t)
        for j in which:
            into[j].start()

    for t in range(count):

        @pl.when(me_ref[0] >= 0)
        def _():
            if t >= 2:
                for copy in copies(t - 2):
                    copy.wait()
            products(t, SPLIT if t == 0 else (0, 1, 2))

        if t == 0:
            for j in range(len(SPLIT), 3):
                pl.when(me_ref[0] >= 0)(functools.partial(products, t, (j,)))

    for sum_ref in sum_refs:
        gate_ref, up_ref = refs[:2]
        cols = slice(begin, begin + count * tile)

        @pl.when(me_ref[0] >= 0)
        def _():
            part = jnp.dot(gate_ref[:, cols], rows(0, begin, count * tile).T, preferred_element_type=F32)
            part += jnp.dot(up_ref[:, cols], rows(1, begin, count * tile).T, preferred_element_type=F32)
            sum_ref[...] = part + refs[2][...] if adds else part

    for t in range(max(count - 2, 0), count):
        for copy in copies(t):
            copy.wait()


def per_device(n_row, n_col, activations, out_grad, w_gate, w_up, w_down):
    share, depth = activations.shape
    hidden = w_gate.shape[1]
    total = share * n_col
    own = total // n_row
    me = lax.axis_index("row").astype(jnp.int32).reshape(1)
    w_gate, w_up, w_down = (pltpu.with_memory_space_constraint(w, pltpu.HBM) for w in (w_gate, w_up, w_down))
    units = hidden // 128
    cuts = [128 * min(-(-units * part // 28), units - (len(CUTS) - 1 - i)) for i, part in enumerate(CUTS)]
    one, two, three, four = ((a, b - a) for a, b in zip(cuts[:-1], cuts[1:]))

    def held(wanted):
        return [vmem((width, depth) if which == 2 else (depth, width), BF16) for which, _, width in wanted]

    mine = pl.pallas_call(
        pair_kernel,
        out_shape=vmem((2 * share, depth), BF16),
        in_specs=[HBM] * 2,
        out_specs=VMEM,
        scratch_shapes=[vmem((2, share, depth), BF16), pltpu.SemaphoreType.DMA((2,))],
        compiler_params=PARAMS,
        name="pair",
    )(*(pltpu.with_memory_space_constraint(x, pltpu.HBM) for x in (activations, out_grad)))
    wanted = ((0, *one), (1, *one), (2, *one))
    gate_one, up_one, down_one, fetched = pl.pallas_call(
        functools.partial(fetch_kernel, wanted),
        out_shape=held(wanted) + [shape((8, 128), F32)],
        in_specs=[SMEM] + [HBM] * 3,
        out_specs=[VMEM] * 4,
        scratch_shapes=[pltpu.SemaphoreType.DMA((3,))],
        compiler_params=PARAMS,
        name="fetch",
    )(me, w_gate, w_up, w_down)
    others = [exchange(mine, "col", n_col, 2 * k) for k in range(1, n_col // 2)]
    near = pl.pallas_call(
        join_kernel,
        out_shape=vmem((n_col * share, depth), BF16),
        in_specs=[VMEM] * (n_col // 2 + 1),
        out_specs=VMEM,
        compiler_params=PARAMS,
        name="join",
    )(mine, *others, fetched)
    far = exchange(near, "col", n_col, 1)
    tokens, grads = pl.pallas_call(
        functools.partial(order_kernel, 2 * share),
        out_shape=[vmem((total, depth), BF16)] * 2,
        in_specs=[SMEM] + [VMEM] * 2,
        out_specs=[VMEM] * 2,
        scratch_shapes=[vmem((2, n_row, own, depth), F32)],
        compiler_params=PARAMS,
        name="order",
    )(me, near, far)

    def forward(start, width, gate, up, down, wanted, after, whole=False):
        weights = (gate, up, down)
        given = tuple(i for i, x in enumerate(weights) if x is not None)
        sends = 0 if whole else n_row - 1
        if whole:
            sums = [vmem((total, 3 * width), F32), vmem((own, 3 * n_row * width), BF16)]
        else:
            sums = [vmem((own, 3 * width), F32)] + [vmem((own, 3 * width), BF16)] * sends
        keep, *rest = pl.pallas_call(
            functools.partial(forward_kernel, start, width, given, wanted, own, sends, tile_of(width)),
            out_shape=sums + held(wanted),
            in_specs=[SMEM] + [VMEM] * (2 + len(given)) + [HBM] * 4,
            out_specs=[VMEM] * (len(sums) + len(wanted)),
            scratch_shapes=([vmem((width, depth), BF16)] if down is None else []) + [pltpu.SemaphoreType.DMA((len(wanted) + 1,))],
            compiler_params=PARAMS,
            name="forward",
        )(me, tokens, grads, *(x for x in weights if x is not None), w_gate, w_up, w_down, after)
        return keep, rest[: len(sums) - 1], rest[len(sums) - 1 :]

    def to_others(blocks):
        return [exchange(x, "row", n_row, s + 1) for s, x in enumerate(blocks)]

    def swiglu(width, keep, got, later, after):
        mine, *sends = pl.pallas_call(
            functools.partial(swiglu_kernel, width, n_row),
            out_shape=[vmem((own, 3 * width), BF16)] + [vmem((own, x.shape[1] + 3 * width), BF16) for x in later],
            in_specs=[HBM] + [VMEM] * (n_row + len(later)),
            out_specs=[VMEM] * (1 + len(later)),
            compiler_params=PARAMS,
            name="swiglu",
        )(after, keep, *got, *later)
        return mine, sends

    def backward(start, width, shift, begin, count, tile, pieces, weights, outs, after, name):
        known = 3 + n_row + len(weights)
        return pl.pallas_call(
            functools.partial(
                backward_kernel, n_row, start, width, shift, begin, count // tile, tile,
                len(weights) + len(outs) + 1, len(weights) > 2,
            ),
            out_shape=[shape((depth, hidden), BF16)] * 2
            + [shape((hidden, depth), BF16)]
            + ([vmem((depth, total), F32)] if weights else []),
            in_specs=[SMEM] + [VMEM] * (known - 1) + [HBM] * (len(outs) + 1),
            out_specs=[HBM] * 3 + ([VMEM] if weights else []),
            input_output_aliases={known + k: k for k in range(len(outs))},
            scratch_shapes=[vmem((2, depth, tile), BF16)] * 2
            + [vmem((2, tile, depth), BF16), pltpu.SemaphoreType.DMA((2, 3))],
            compiler_params=PARAMS,
            name=name,
        )(me, turned, grads, *pieces, *weights, *outs, after)

    keep_one, sends, (gate_two,) = forward(*one, gate_one, up_one, down_one, ((0, *two),), me)
    got_one = to_others(sends)
    turned = pl.pallas_call(
        turn_kernel,
        out_shape=vmem((depth, total), BF16),
        in_specs=[VMEM, HBM],
        out_specs=VMEM,
        compiler_params=PARAMS,
        name="turn",
    )(tokens, keep_one)
    keep_two, sends, (up_two,) = forward(*two, gate_two, None, None, ((1, *two),), turned)
    mine_one, sends = swiglu(one[1], keep_one, got_one, sends, me)
    got_two = to_others(sends)
    keep_three, sends, (gate_three, up_three, gate_four, up_four, down_four) = forward(
        *three, None, None, None, ((0, *three), (1, *three), (0, *four), (1, *four), (2, *four)), mine_one
    )
    mine_two, sends = swiglu(two[1], keep_two, got_two, sends, me)
    got_three = to_others(sends)
    keep_four, sends, _ = forward(*four, gate_four, up_four, down_four, (), mine_two, whole=True)
    *outs, grad_input = backward(
        *one, 3 * two[1], 0, one[1], tile_of(one[1]), [mine_one, *got_two], (gate_one, up_one), (), mine_two, "backward_one"
    )
    mine_three, sends = swiglu(three[1], keep_three, got_three, sends, grad_input)
    got_four = to_others(sends * (n_row - 1))
    *outs, grad_input = backward(
        *two, 3 * three[1], 0, two[1], tile_of(two[1]), [mine_two, *got_three], (gate_two, up_two, grad_input), outs, mine_three, "backward_two"
    )
    pieces = [mine_three, *got_four]
    pieces_four = pl.pallas_call(
        functools.partial(swiglu_all_kernel, four[1], n_row),
        out_shape=[vmem((own, 3 * four[1]), BF16)] * n_row,
        in_specs=[HBM] + [VMEM] * n_row,
        out_specs=[VMEM] * n_row,
        compiler_params=PARAMS,
        name="swiglu_all",
    )(grad_input, keep_four, *got_four)
    shift = 3 * n_row * four[1]
    grad_input = pl.pallas_call(
        functools.partial(input_kernel, n_row, ((three[1], shift), (four[1], 0))),
        out_shape=vmem((total, depth), F32),
        in_specs=[SMEM] + [VMEM] * (2 * n_row + 5),
        out_specs=VMEM,
        compiler_params=PARAMS,
        name="input_grad",
    )(me, *pieces, *pieces_four, gate_three, up_three, gate_four, up_four, grad_input)
    blocks = grad_input.reshape(n_col // 2, 2, share, depth)
    outs = backward(*four, 0, 0, four[1], tile_of(four[1], 256), pieces_four, (), outs, grad_input, "weight_grads_early")
    other = exchange(blocks[:, 1], "col", n_col, 1)
    other, *outs = lax.optimization_barrier((other, *outs))
    summed = blocks[:, 0] + other
    outs = backward(*three, shift, 0, three[1], tile_of(three[1], 256), pieces, (), outs, summed, "weight_grads")
    result = summed[0]
    for k in range(1, n_col // 2):
        result = result + exchange(summed[k], "col", n_col, 2 * k)
    return (result.astype(BF16), *outs)


def solution(mesh):
    in_specs = (P("col", "row"), P("col", "row"), P("row", "col"), P("row", "col"), P("col", "row"))
    out_specs = (P("col", "row"), P("row", "col"), P("row", "col"), P("col", "row"))
    return jax.shard_map(
        functools.partial(per_device, mesh.shape["row"], mesh.shape["col"]),
        mesh=mesh,
        in_specs=in_specs,
        out_specs=out_specs,
        check_vma=False,
    )
```

```python
import functools

import jax
import jax.numpy as jnp
from jax import lax
from jax.experimental import pallas as pl
from jax.experimental.pallas import tpu as pltpu
from jax.sharding import PartitionSpec as P

BF16, F32 = jnp.bfloat16, jnp.float32
HBM = pl.BlockSpec(memory_space=pl.ANY)
VMEM = pl.BlockSpec(memory_space=pltpu.VMEM)
SMEM = pl.BlockSpec(memory_space=pltpu.SMEM)
CONTRACT_LAST = (((1,), (1,)), ((), ()))
CONTRACT_FIRST = (((0,), (0,)), ((), ()))
CUTS = (0, 8, 16, 26, 28)
SPLIT = (0, 1, 2)
PARAMS = pltpu.CompilerParams(vmem_limit_bytes=15 << 20)
vmem = pltpu.VMEM
shape = jax.ShapeDtypeStruct


def exchange(x, axis, size, offset):
    return lax.ppermute(x, axis, [(i, i ^ offset) for i in range(size)])


def tile_of(width, most=512):
    return next(t for t in (512, 256, 128) if t <= most and width % t == 0)


def tiles(width, tile):
    return [(at, min(tile, width - at)) for at in range(0, width, tile)]


def pair_kernel(first_hbm, second_hbm, out_ref, both, sems):
    copies = [pltpu.make_async_copy(x, both.at[i], sems.at[i]) for i, x in enumerate((first_hbm, second_hbm))]
    for copy in copies:
        copy.start()
    for copy in copies:
        copy.wait()
    out_ref[...] = jnp.concatenate([both[0], both[1]], axis=0)


def join_kernel(*refs):
    rows = refs[0].shape[0]
    for i, ref in enumerate(refs[:-2]):
        refs[-1][i * rows : (i + 1) * rows, :] = ref[...]


def order_kernel(rows, me_ref, mine_ref, other_ref, tokens_ref, grads_ref, turned_ref, scratch):
    me = me_ref[0]
    share = rows // 2
    n = mine_ref.shape[0] // rows
    total = tokens_ref.shape[0]
    per_row = total // scratch.shape[1]
    for half, out in ((0, tokens_ref), (1, grads_ref)):
        for k in range(n):
            for c, ref in ((0, mine_ref), (1, other_ref)):
                block = ref[k * rows : (k + 1) * rows, :].astype(F32)
                at = (2 * k + c) * share
                scratch[half, at // per_row, at % per_row : at % per_row + share, :] = block[
                    half * share : (half + 1) * share
                ]
        parts = [scratch[half, k ^ me] for k in range(scratch.shape[1])]
        rows_in_order = jnp.concatenate(parts, axis=0)
        out[...] = rows_in_order.astype(BF16)
        if half == 0:
            turned_ref[...] = rows_in_order.T.astype(BF16)


def weights_copies(sources, wanted, targets, sems):
    copies = []
    for i, ((which, start, width), target) in enumerate(zip(wanted, targets)):
        part = pl.ds(start, width)
        source = sources[which].at[part] if which == 2 else sources[which].at[:, part]
        copies.append(pltpu.make_async_copy(source, target, sems.at[i]))
    return copies


def fetch_kernel(wanted, me_ref, *refs):
    sources, targets, (done_ref, sems) = refs[:3], refs[3:-2], refs[-2:]
    copies = weights_copies(sources, wanted, targets, sems)
    for copy in copies:
        copy.start()
    done_ref[...] = jnp.zeros_like(done_ref)
    for copy in copies:
        copy.wait()


def forward_kernel(start, width, given, wanted, own, sends, tile, me_ref, tokens_ref, grads_ref, *refs):
    weights, refs = dict(zip(given, refs)), refs[len(given) :]
    sources, refs = refs[:3], refs[4:]
    keep_ref, send_refs, refs = refs[0], refs[1 : 1 + max(sends, 1)], refs[1 + max(sends, 1) :]
    send_ref = send_refs[0]
    targets, refs = refs[: len(wanted)], refs[len(wanted) :]
    streamed = [which for which in (0, 2, 1) if which not in given]
    if 2 in streamed:
        wanted, targets = ((2, start, width), *wanted), (refs[0], *targets)
    pairs = sorted(zip(wanted, targets), key=lambda p: streamed.index(p[0][0]) if p[0] == (p[0][0], start, width) else 3)
    copies = weights_copies(sources, [p[0] for p in pairs], [p[1] for p in pairs], refs[-1])
    for copy in copies:
        copy.start()
    for which, (_, target) in zip(streamed, pairs):
        weights[which] = target

    def put(i, at, part):
        to = i * width + at
        if sends == 0:
            keep_ref[:, to : to + tile] = part
            for k in range(part.shape[0] // own):
                send_ref[:, 3 * k * width + to : 3 * k * width + to + tile] = part[k * own : (k + 1) * own].astype(BF16)
        else:
            keep_ref[:, to : to + tile] = part[:own]
            for s, ref in enumerate(send_refs):
                ref[:, to : to + tile] = part[(s + 1) * own : (s + 2) * own].astype(BF16)

    def product(which):
        for at in range(0, width, tile):
            if which == 2:
                down = weights[2][at : at + tile, :]
                put(2, at, lax.dot_general(grads_ref[...], down, CONTRACT_LAST, preferred_element_type=F32))
            else:
                columns = weights[which][:, at : at + tile]
                put(which, at, jnp.dot(tokens_ref[...], columns, preferred_element_type=F32))

    if given:

        @pl.when(me_ref[0] >= 0)
        def _():
            for which in given:
                product(which)

    for which, copy in zip(streamed, copies):
        copy.wait()
        pl.when(me_ref[0] >= 0)(functools.partial(product, which))
    for copy in copies[len(streamed) :]:
        copy.wait()


def gradients(sums, width):
    gate, upward, back = (sums[:, i * width : (i + 1) * width] for i in range(3))
    sigma = 1.0 / (1.0 + jnp.exp(-gate))
    return back * upward * sigma * (1.0 + gate * (1.0 - sigma)), back * gate * sigma, gate * sigma * upward


def swiglu_kernel(width, n, after_ref, keep_ref, *refs):
    pieces, refs = refs[: n - 1], refs[n - 1 :]
    later, out_ref, send_refs = refs[: len(refs) // 2], refs[len(refs) // 2], refs[len(refs) // 2 + 1 :]
    sums = keep_ref[...]
    for ref in pieces:
        sums = sums + ref[:, : 3 * width].astype(F32)
    for i, part in enumerate(gradients(sums, width)):
        out_ref[:, i * width : (i + 1) * width] = part.astype(BF16)
    for before, after in zip(later, send_refs):
        split = before.shape[1]
        after[:, :split] = before[...]
        after[:, split:] = out_ref[...]


def swiglu_all_kernel(width, n, after_ref, keep_ref, *refs):
    pieces, out_refs = refs[: n - 1], refs[n - 1 :]
    own = out_refs[0].shape[0]
    for k, out_ref in enumerate(out_refs):
        sums = keep_ref[k * own : (k + 1) * own, :]
        for s, ref in enumerate(pieces):
            at = 3 * (k ^ (s + 1)) * width
            sums = sums + ref[:, at : at + 3 * width].astype(F32)
        for i, part in enumerate(gradients(sums, width)):
            out_ref[:, i * width : (i + 1) * width] = part.astype(BF16)


def input_kernel(n, chunks, me_ref, *refs):
    sum_ref, out_ref = refs[-2:]
    products = []
    for i, (width, shift) in enumerate(chunks):
        mine_ref, *pieces = refs[i * n : (i + 1) * n]
        weights = refs[n * len(chunks) + 2 * i : n * len(chunks) + 2 * i + 2]
        for j, ref in enumerate(weights):
            cols = slice(j * width, (j + 1) * width)
            others = [r[:, shift + j * width : shift + (j + 1) * width] for r in pieces]
            products.append((ref, jnp.concatenate([mine_ref[:, cols]] + others, axis=0).T))
    own = refs[0].shape[0]
    for at, size in tiles(sum_ref.shape[0], 2048):
        rows = slice(at, at + size)
        part = sum_ref[rows, :]
        for ref, grads in products:
            part += jnp.dot(ref[rows, :], grads, preferred_element_type=F32)
        part = part.T
        for k in range(n):
            out_ref[pl.ds(pl.multiple_of((k ^ me_ref[0]) * own, 8), own), rows] = part[k * own : (k + 1) * own]


def backward_kernel(n, start, width, shift, begin, count, tile, n_in, adds, me_ref, turned_ref, grads_ref, *refs):
    mine_ref, pieces, refs = refs[0], refs[1:n], refs[n:]
    bufs, sems = refs[-4:-1], refs[-1]
    outs, sum_refs = refs[n_in : n_in + 3], refs[n_in + 3 : -4]

    def rows(j, at, size):
        cols = j * width + at
        parts = [mine_ref[:, cols : cols + size]] + [r[:, shift + cols : shift + cols + size] for r in pieces]
        return jnp.concatenate(parts, axis=0)

    def copies(t):
        to = pl.ds(start + begin + t * tile, tile)
        targets = (outs[0].at[:, to], outs[1].at[:, to], outs[2].at[to])
        return [pltpu.make_async_copy(b.at[t % 2], o, sems.at[t % 2, j]) for j, (b, o) in enumerate(zip(bufs, targets))]

    def products(t, which):
        at = begin + t * tile
        for j in which:
            if j == 2:
                part = lax.dot_general(rows(2, at, tile), grads_ref[...], CONTRACT_FIRST, preferred_element_type=F32)
            else:
                part = jnp.dot(turned_ref[...], rows(j, at, tile), preferred_element_type=F32)
            bufs[j][t % 2] = part.astype(BF16)
        into = copies(t)
        for j in which:
            into[j].start()

    for t in range(count):

        @pl.when(me_ref[0] >= 0)
        def _():
            if t >= 2:
                for copy in copies(t - 2):
                    copy.wait()
            products(t, SPLIT if t == 0 else (0, 1, 2))

        if t == 0:
            for j in range(len(SPLIT), 3):
                pl.when(me_ref[0] >= 0)(functools.partial(products, t, (j,)))

    for sum_ref in sum_refs:
        gate_ref, up_ref = refs[:2]
        cols = slice(begin, begin + count * tile)

        @pl.when(me_ref[0] >= 0)
        def _():
            part = jnp.dot(gate_ref[:, cols], rows(0, begin, count * tile).T, preferred_element_type=F32)
            part += jnp.dot(up_ref[:, cols], rows(1, begin, count * tile).T, preferred_element_type=F32)
            sum_ref[...] = part + refs[2][...] if adds else part

    for t in range(max(count - 2, 0), count):
        for copy in copies(t):
            copy.wait()


def per_device(n_row, n_col, activations, out_grad, w_gate, w_up, w_down):
    share, depth = activations.shape
    hidden = w_gate.shape[1]
    total = share * n_col
    own = total // n_row
    me = lax.axis_index("row").astype(jnp.int32).reshape(1)
    w_gate, w_up, w_down = (pltpu.with_memory_space_constraint(w, pltpu.HBM) for w in (w_gate, w_up, w_down))
    units = hidden // 128
    cuts = [128 * min(-(-units * part // 28), units - (len(CUTS) - 1 - i)) for i, part in enumerate(CUTS)]
    one, two, three, four = ((a, b - a) for a, b in zip(cuts[:-1], cuts[1:]))

    def held(wanted):
        return [vmem((width, depth) if which == 2 else (depth, width), BF16) for which, _, width in wanted]

    mine = pl.pallas_call(
        pair_kernel,
        out_shape=vmem((2 * share, depth), BF16),
        in_specs=[HBM] * 2,
        out_specs=VMEM,
        scratch_shapes=[vmem((2, share, depth), BF16), pltpu.SemaphoreType.DMA((2,))],
        compiler_params=PARAMS,
        name="pair",
    )(*(pltpu.with_memory_space_constraint(x, pltpu.HBM) for x in (activations, out_grad)))
    wanted = ((0, *one), (1, *one), (2, *one))
    gate_one, up_one, down_one, fetched = pl.pallas_call(
        functools.partial(fetch_kernel, wanted),
        out_shape=held(wanted) + [shape((8, 128), F32)],
        in_specs=[SMEM] + [HBM] * 3,
        out_specs=[VMEM] * 4,
        scratch_shapes=[pltpu.SemaphoreType.DMA((3,))],
        compiler_params=PARAMS,
        name="fetch",
    )(me, w_gate, w_up, w_down)
    others = [exchange(mine, "col", n_col, 2 * k) for k in range(1, n_col // 2)]
    near = pl.pallas_call(
        join_kernel,
        out_shape=vmem((n_col * share, depth), BF16),
        in_specs=[VMEM] * (n_col // 2 + 1),
        out_specs=VMEM,
        compiler_params=PARAMS,
        name="join",
    )(mine, *others, fetched)
    far = exchange(near, "col", n_col, 1)
    tokens, grads, turned = pl.pallas_call(
        functools.partial(order_kernel, 2 * share),
        out_shape=[vmem((total, depth), BF16)] * 2 + [vmem((depth, total), BF16)],
        in_specs=[SMEM] + [VMEM] * 2,
        out_specs=[VMEM] * 3,
        scratch_shapes=[vmem((2, n_row, own, depth), F32)],
        compiler_params=PARAMS,
        name="order",
    )(me, near, far)

    def forward(start, width, gate, up, down, wanted, after, whole=False):
        weights = (gate, up, down)
        given = tuple(i for i, x in enumerate(weights) if x is not None)
        sends = 0 if whole else n_row - 1
        if whole:
            sums = [vmem((total, 3 * width), F32), vmem((own, 3 * n_row * width), BF16)]
        else:
            sums = [vmem((own, 3 * width), F32)] + [vmem((own, 3 * width), BF16)] * sends
        keep, *rest = pl.pallas_call(
            functools.partial(forward_kernel, start, width, given, wanted, own, sends, tile_of(width)),
            out_shape=sums + held(wanted),
            in_specs=[SMEM] + [VMEM] * (2 + len(given)) + [HBM] * 4,
            out_specs=[VMEM] * (len(sums) + len(wanted)),
            scratch_shapes=([vmem((width, depth), BF16)] if down is None else []) + [pltpu.SemaphoreType.DMA((len(wanted) + 1,))],
            compiler_params=PARAMS,
            name="forward",
        )(me, tokens, grads, *(x for x in weights if x is not None), w_gate, w_up, w_down, after)
        return keep, rest[: len(sums) - 1], rest[len(sums) - 1 :]

    def to_others(blocks):
        return [exchange(x, "row", n_row, s + 1) for s, x in enumerate(blocks)]

    def swiglu(width, keep, got, later, after):
        mine, *sends = pl.pallas_call(
            functools.partial(swiglu_kernel, width, n_row),
            out_shape=[vmem((own, 3 * width), BF16)] + [vmem((own, x.shape[1] + 3 * width), BF16) for x in later],
            in_specs=[HBM] + [VMEM] * (n_row + len(later)),
            out_specs=[VMEM] * (1 + len(later)),
            compiler_params=PARAMS,
            name="swiglu",
        )(after, keep, *got, *later)
        return mine, sends

    def backward(start, width, shift, begin, count, tile, pieces, weights, outs, after, name):
        known = 3 + n_row + len(weights)
        return pl.pallas_call(
            functools.partial(
                backward_kernel, n_row, start, width, shift, begin, count // tile, tile,
                len(weights) + len(outs) + 1, len(weights) > 2,
            ),
            out_shape=[shape((depth, hidden), BF16)] * 2
            + [shape((hidden, depth), BF16)]
            + ([vmem((depth, total), F32)] if weights else []),
            in_specs=[SMEM] + [VMEM] * (known - 1) + [HBM] * (len(outs) + 1),
            out_specs=[HBM] * 3 + ([VMEM] if weights else []),
            input_output_aliases={known + k: k for k in range(len(outs))},
            scratch_shapes=[vmem((2, depth, tile), BF16)] * 2
            + [vmem((2, tile, depth), BF16), pltpu.SemaphoreType.DMA((2, 3))],
            compiler_params=PARAMS,
            name=name,
        )(me, turned, grads, *pieces, *weights, *outs, after)

    keep_one, sends, (gate_two,) = forward(*one, gate_one, up_one, down_one, ((0, *two),), me)
    got_one = to_others(sends)
    keep_two, sends, (up_two,) = forward(*two, gate_two, None, None, ((1, *two),), me)
    mine_one, sends = swiglu(one[1], keep_one, got_one, sends, me)
    got_two = to_others(sends)
    keep_three, sends, (gate_three, up_three, gate_four, up_four, down_four) = forward(
        *three, None, None, None, ((0, *three), (1, *three), (0, *four), (1, *four), (2, *four)), mine_one
    )
    mine_two, sends = swiglu(two[1], keep_two, got_two, sends, me)
    got_three = to_others(sends)
    keep_four, sends, _ = forward(*four, gate_four, up_four, down_four, (), mine_two, whole=True)
    *outs, grad_input = backward(
        *one, 3 * two[1], 0, one[1], tile_of(one[1]), [mine_one, *got_two], (gate_one, up_one), (), mine_two, "backward_one"
    )
    mine_three, sends = swiglu(three[1], keep_three, got_three, sends, grad_input)
    got_four = to_others(sends * (n_row - 1))
    *outs, grad_input = backward(
        *two, 3 * three[1], 0, two[1], tile_of(two[1]), [mine_two, *got_three], (gate_two, up_two, grad_input), outs, mine_three, "backward_two"
    )
    pieces = [mine_three, *got_four]
    pieces_four = pl.pallas_call(
        functools.partial(swiglu_all_kernel, four[1], n_row),
        out_shape=[vmem((own, 3 * four[1]), BF16)] * n_row,
        in_specs=[HBM] + [VMEM] * n_row,
        out_specs=[VMEM] * n_row,
        compiler_params=PARAMS,
        name="swiglu_all",
    )(grad_input, keep_four, *got_four)
    shift = 3 * n_row * four[1]
    grad_input = pl.pallas_call(
        functools.partial(input_kernel, n_row, ((three[1], shift), (four[1], 0))),
        out_shape=vmem((total, depth), F32),
        in_specs=[SMEM] + [VMEM] * (2 * n_row + 5),
        out_specs=VMEM,
        compiler_params=PARAMS,
        name="input_grad",
    )(me, *pieces, *pieces_four, gate_three, up_three, gate_four, up_four, grad_input)
    blocks = grad_input.reshape(n_col // 2, 2, share, depth)
    outs = backward(*four, 0, 0, four[1], tile_of(four[1], 256), pieces_four, (), outs, grad_input, "weight_grads_early")
    other = exchange(blocks[:, 1], "col", n_col, 1)
    other, *outs = lax.optimization_barrier((other, *outs))
    summed = blocks[:, 0] + other
    outs = backward(*three, shift, 0, three[1], tile_of(three[1], 256), pieces, (), outs, summed, "weight_grads")
    result = summed[0]
    for k in range(1, n_col // 2):
        result = result + exchange(summed[k], "col", n_col, 2 * k)
    return (result.astype(BF16), *outs)


def solution(mesh):
    in_specs = (P("col", "row"), P("col", "row"), P("row", "col"), P("row", "col"), P("col", "row"))
    out_specs = (P("col", "row"), P("row", "col"), P("row", "col"), P("col", "row"))
    return jax.shard_map(
        functools.partial(per_device, mesh.shape["row"], mesh.shape["col"]),
        mesh=mesh,
        in_specs=in_specs,
        out_specs=out_specs,
        check_vma=False,
    )
```
